32 devices in a mesh: tile: 8 (over z, y), sub: 4 (over x, core).
Axes of the slice: x: 2, y: 2, z: 4, core: 2. Of those that a mesh axis runs over, the one named last changes fastest.
Arguments:
- atm_fields: float32 [6, 256, 128], P(None, ('tile', 'sub')), may hold values from -6 to 6
- pair_atm: int32 [640], P(('tile', 'sub')), may hold values from 0 to 7
- pair_land: int32 [640], P(('tile', 'sub')), may hold values from 0 to 511, as said below
- pair_weight: bfloat16 [640, 3, 128, 512], P(('tile', 'sub')), may hold values from -0.3125 to 0.3125
- land_mask: int32 [262144], P(('tile', 'sub')), may hold values 0 or 1
- conductance: float32 [20, 262144], P(None, ('tile', 'sub')), may hold values from 0.1 to 3
- soil_moisture: float32 [20, 262144], P(None, ('tile', 'sub')), may hold values from 0.1 to 0.5
- river_owner: int32 [2048], P(('tile', 'sub')), may hold values from 0 to 7, as said below
Outputs:
- land_forcing: bfloat16 [6, 262144], P(None, ('tile', 'sub'))
- soil_state: float32 [20, 262144], P(None, ('tile', 'sub'))
- river_runoff: float32 [8, 4, 8, 16, 128], P('tile', 'sub')
- river_blocks: int32 [8, 4, 8, 16], P('tile', 'sub')
The draws below stay inside these ranges and needn't reach their ends.
Inputs may be any that keep to these rules, and one draw needn't show every extreme that they name: `pair_land`: the land block of a pair lies in the tile of the pair's atmosphere device or in one of the two tiles beside it, cyclically over the 8 tiles (device d = t * 4 + s owns land blocks d * 16 onward). At most 4 pairs of one device name land blocks of one device, and in every tile some land device receives exactly 4 pairs from each of the tile's 4 devices. `river_owner`: A block goes to the river owner device on the given tile with the same sub index. At most 16 blocks of one device go to one owner, and for every sub index some owner receives exactly 16 blocks from each device of that sub index.
All inputs are finite; a program needn't handle non-finite values. No bound on the sum of `land_mask` on one device may be relied on, other than what follows from the above.
Results may differ from the reference program's by a relative error of at most 0.0049.
Values sent between devices are 32-bit elements; how exact they have to be, the bound alone decides.
A program may use at most 64 MiB of HBM per device.

```python
import math
import jax
import jax.numpy as jnp
from jax import lax

F = 6
SOIL = 20
SOIL_STEPS = 4
AX = 128
LBLK = 512
RBLK = 128
CAP_P = 4
AROWS = 8
PAIRS_DEV = 20
LB_DEV = 16
RB_DEV = 64
CAP_R = 16
ATM_ROWS = 256
PAIRS = 640
LAND_BLOCKS = 512
LAND = 262144
N_TILE = 8
N_SUB = 4


def spread_slots(key, row_count, group_count, capacity, count, forced):
    first_key, second_key = jax.random.split(key)
    slot_total = group_count * capacity
    orders = jax.vmap(lambda k: jax.random.permutation(k, slot_total))(jax.random.split(first_key, row_count))
    orders = orders.astype(jnp.int32)
    inside = (orders // capacity == forced[:, None]).astype(jnp.int32)
    placing = jnp.argsort(inside, axis=1, stable=True)
    others = jnp.take_along_axis(orders, placing, axis=1)[:, :count - capacity]
    fixed_part = forced[:, None] * capacity + jnp.arange(capacity, dtype=jnp.int32)[None, :]
    chosen = jnp.concatenate([fixed_part, others], axis=1)
    shuffle = jax.vmap(lambda k: jax.random.permutation(k, count))(jax.random.split(second_key, row_count))
    chosen = jnp.take_along_axis(chosen, shuffle.astype(jnp.int32), axis=1)
    return chosen // capacity


def draw_pair_land(key, part):
    devices = N_TILE * N_SUB
    first_key, second_key, third_key = jax.random.split(jax.random.fold_in(key, 11), 3)
    forced_tile = jax.random.randint(first_key, (N_TILE,), 0, 3 * N_SUB, dtype=jnp.int32)
    forced = jnp.repeat(forced_tile, N_SUB)
    group_id = spread_slots(second_key, devices, 3 * N_SUB, CAP_P, PAIRS_DEV, forced)
    local_block = jax.random.randint(third_key, (devices, PAIRS_DEV), 0, LB_DEV, dtype=jnp.int32)
    tile_index = (jnp.arange(devices, dtype=jnp.int32) // N_SUB)[:, None]
    dest_tile = (tile_index + group_id // N_SUB - 1 + N_TILE) % N_TILE
    land_block = (dest_tile * N_SUB + group_id % N_SUB) * LB_DEV + local_block
    return land_block.reshape(-1).astype(jnp.int32)


def draw_river_owner(key, part):
    devices = N_TILE * N_SUB
    first_key, second_key = jax.random.split(jax.random.fold_in(key, 23))
    forced_sub = jax.random.randint(first_key, (N_SUB,), 0, N_TILE, dtype=jnp.int32)
    forced = jnp.tile(forced_sub, N_TILE)
    owners = spread_slots(second_key, devices, N_TILE, CAP_R, RB_DEV, forced)
    return owners.reshape(-1).astype(jnp.int32)


def with_ends(drawn, stream_key, smallest, high):
    index_at = [jax.random.randint(jax.random.fold_in(stream_key, axis), (), 0, length) for axis, length in enumerate(drawn.shape)]
    main_axis = drawn.shape.index(max(drawn.shape))
    beside = index_at[:main_axis] + [(index_at[main_axis] + 1) % drawn.shape[main_axis]] + index_at[main_axis + 1:]
    return drawn.at[tuple(index_at)].set(smallest).at[tuple(beside)].set(high)


def shard_levels(own_key, shape, shards, least, largest):
    def one(dim, shards_of):
        draws = jax.random.uniform(jax.random.fold_in(jax.random.fold_in(own_key, 6), dim), (shards_of,), jnp.float32, least / len(shards), largest / len(shards))
        return jnp.repeat(jnp.exp(draws), shape[dim] // shards_of).reshape((-1,) + (1,) * (len(shape) - dim - 1))

    loudness = one(*shards[0])
    for cut in shards[1:]:
        loudness = loudness * one(*cut)
    return loudness


def centred(rng, shape, width, bound, cuts=(), kind=jnp.bfloat16):
    result = jax.random.normal(rng, shape, jnp.float32) * width
    if len(cuts) > 0:
        result = shard_levels(rng, shape, cuts, -0.22, 0.18) * result
    return jnp.clip(result, min=-bound, max=bound).astype(kind)


def setup_inputs(seed: int = 0) -> dict:
    streams_of = jax.random.split(jax.random.key(seed), 9)
    atm_fields = centred(streams_of[0], (F, ATM_ROWS, AX), 1.0, 6.0, ((1, 32),), jnp.float32)
    pair_atm = with_ends(jax.random.randint(streams_of[1], (PAIRS,), 0, AROWS), jax.random.fold_in(streams_of[1], 1), 0, AROWS - 1).astype(jnp.int32)
    pair_land = draw_pair_land(jax.random.fold_in(streams_of[8], 71), 0)
    pair_weight = centred(streams_of[3], (PAIRS, 3, AX, LBLK), (3 * AX) ** -0.5, 0.3125, ((0, 32),))
    land_mask = with_ends((jax.random.randint(streams_of[4], (LAND,), 0, 10) < 7).astype(jnp.int32), jax.random.fold_in(streams_of[4], 1), 0, 1)
    conductance = jnp.clip(jnp.exp(math.log(3.0) - 3.4011974 * jax.random.uniform(streams_of[5], (SOIL, LAND), jnp.float32) ** shard_levels(streams_of[5], (SOIL, LAND), ((1, 32),), -0.2, 0.2)), 0.1, 3.0)
    soil_moisture = jnp.clip(0.1 + 0.4 * jax.random.uniform(streams_of[6], (SOIL, LAND), jnp.float32) ** shard_levels(streams_of[6], (SOIL, LAND), ((1, 32),), -0.2, 0.2), 0.1, 0.5)
    river_owner = draw_river_owner(jax.random.fold_in(streams_of[8], 71), 0)
    return dict(atm_fields=atm_fields, pair_atm=pair_atm, pair_land=pair_land, pair_weight=pair_weight, land_mask=land_mask, conductance=conductance, soil_moisture=soil_moisture, river_owner=river_owner)


def x_gradient(fields):
    inner = (fields[:, :, 2:] - fields[:, :, :-2]) * 0.5
    first = fields[:, :, 1:2] - fields[:, :, 0:1]
    last = fields[:, :, -1:] - fields[:, :, -2:-1]
    return jnp.concatenate([first, inner, last], axis=2)


def column_factors(conductance):
    layers = conductance.shape[0]
    inverse = []
    ratios = []
    for k in range(layers):
        diagonal = 1.0 + conductance[k]
        if k > 0:
            diagonal = diagonal + conductance[k - 1] - conductance[k - 1] * conductance[k - 1] * inverse[k - 1]
        pivot_inv = 1.0 / diagonal
        inverse.append(pivot_inv)
        ratios.append(-conductance[k] * pivot_inv)
    return inverse, ratios


def column_solve(moisture, source, conductance, inverse, ratios):
    layers = len(inverse)
    forward = []
    for k in range(layers):
        if k == 0:
            column_value = moisture[0] + source
        else:
            column_value = moisture[k] + conductance[k - 1] * forward[k - 1]
        forward.append(column_value * inverse[k])
    solved = [forward[layers - 1]]
    for k in range(layers - 2, -1, -1):
        solved.insert(0, forward[k] - ratios[k] * solved[0])
    return jnp.stack(solved)


def soil_update(forcing, land_mask, conductance, soil_moisture):
    wetness = land_mask.astype(jnp.float32)
    source = wetness * (jax.nn.softplus(forcing[0]) * jax.nn.sigmoid(forcing[1])
                        - 0.5 * jax.nn.sigmoid(forcing[2]) * jax.nn.softplus(forcing[3]))
    surface = wetness * jax.nn.softplus(forcing[0]) * (1.0 - jax.nn.sigmoid(forcing[1]))
    inverse, ratios = column_factors(conductance)
    bottom = conductance.shape[0] - 1
    moisture = soil_moisture
    drainage = jnp.zeros_like(surface)
    for substep in range(SOIL_STEPS):
        moisture = column_solve(moisture, source, conductance, inverse, ratios)
        drainage = drainage + conductance[bottom] * moisture[bottom]
    runoff = wetness * (SOIL_STEPS * surface + drainage)
    return moisture, runoff


def reference(atm_fields, pair_atm, pair_land, pair_weight, land_mask, conductance, soil_moisture, river_owner):
    devices = N_TILE * N_SUB
    grad_x = x_gradient(atm_fields)
    grad_y = (jnp.roll(atm_fields, -1, 1) - jnp.roll(atm_fields, 1, 1)) * 0.5
    stacked = jnp.concatenate([atm_fields, grad_x, grad_y], axis=2).astype(jnp.bfloat16)
    stacked_dev = stacked.reshape(F, devices, AROWS, 3 * AX).transpose(1, 0, 2, 3)
    atm_dev = pair_atm.reshape(devices, PAIRS_DEV)
    weight_dev = pair_weight.reshape(devices, PAIRS_DEV, 3 * AX, LBLK)

    def one_device(inputs):
        device_rows, row_index, weights = inputs
        picked = device_rows[:, row_index, :].astype(jnp.float32)
        return jnp.einsum('fpk,pkl->pfl', picked, weights.astype(jnp.float32))

    partial_value = lax.map(one_device, (stacked_dev, atm_dev, weight_dev))
    blocks = jnp.zeros((LAND_BLOCKS, F, LBLK), jnp.float32).at[pair_land].add(partial_value.reshape(PAIRS, F, LBLK))
    forcing = blocks.transpose(1, 0, 2).reshape(F, LAND)
    land_forcing = forcing.astype(jnp.bfloat16)
    moisture, runoff = soil_update(forcing, land_mask, conductance, soil_moisture)

    runoff_blocks = runoff.reshape(devices, RB_DEV, RBLK)
    owners = river_owner.reshape(devices, RB_DEV)
    hits = (owners[:, :, None] == jnp.arange(N_TILE, dtype=jnp.int32)[None, None, :]).astype(jnp.int32)
    earlier = jnp.cumsum(hits, axis=1) - hits
    ranks = jnp.sum(earlier * hits, axis=2).astype(jnp.int32)
    slots = (owners * CAP_R + ranks).astype(jnp.int32)
    device_ids = jnp.arange(devices, dtype=jnp.int32)[:, None]
    block_ids = jnp.arange(devices * RB_DEV, dtype=jnp.int32).reshape(devices, RB_DEV)
    values = jnp.zeros((devices, N_TILE * CAP_R, RBLK), jnp.float32).at[device_ids, slots].set(runoff_blocks)
    numbers = jnp.full((devices, N_TILE * CAP_R), -1, jnp.int32).at[device_ids, slots].set(block_ids)
    river_runoff = values.reshape(N_TILE, N_SUB, N_TILE, CAP_R, RBLK).transpose(2, 1, 0, 3, 4)
    river_blocks = numbers.reshape(N_TILE, N_SUB, N_TILE, CAP_R).transpose(2, 1, 0, 3)
    return (land_forcing, moisture, river_runoff, river_blocks)
```

```python
import functools

import jax
import jax.numpy as jnp
from jax import lax
from jax.experimental import pallas as pl
from jax.experimental.pallas import tpu as pltpu
from jax.sharding import PartitionSpec as P

MESH = pl.DeviceIdType.MESH
SOIL_STEPS = 4
LB_DEV = 16
CAP_P = 4
LANES = 128
SUBL = 8
CHUNKS = 2
WPARTS = 4
f32 = jnp.float32
bf16 = jnp.bfloat16
i32 = jnp.int32


def iota(shape, dim):
    return lax.broadcasted_iota(i32, shape, dim)


def split_dot(onehot, values):
    high = values.astype(bf16)
    low = (values - high.astype(f32)).astype(bf16)
    return jnp.dot(onehot, high, preferred_element_type=f32) + jnp.dot(
        onehot, low, preferred_element_type=f32
    )


def swap8(regs):
    row = iota((SUBL, LANES), 0)
    regs = list(regs)
    for step in (1, 2, 4):
        keep = (row & step) == 0
        out = list(regs)
        for i in range(8):
            if i & step == 0:
                a, b = regs[i], regs[i + step]
                out[i] = jnp.where(keep, a, pltpu.roll(b, step, 0))
                out[i + step] = jnp.where(keep, pltpu.roll(a, SUBL - step, 0), b)
        regs = out
    return regs


def softplus(x):
    return jnp.maximum(x, 0.0) + jnp.log1p(jnp.exp(-jnp.abs(x)))


def sigmoid(x):
    return 1.0 / (1.0 + jnp.exp(-x))


def kernel(
    tiles, subs, capacity, atm, pair_atm, pair_land, owner, mask, w_hbm, c_hbm, m_hbm,
    forcing_out, soil_out, river_out, number_out,
    w_v, c_raw, m_raw, ct, mt, gt, rt, it, fwd, soil_v, edge_s, edge_r, meta_s, meta_r, slot_s, slot_r,
    num_s, num_r, val_s, val_r, picked, pbuf, amat, bmat, rmat, runoff,
    w_sem, cm_sem, out_sem, edge_ss, edge_rs, meta_ss, meta_rs, slot_ss, slot_rs,
    num_ss, num_rs, val_ss, val_rs,
):
    t = lax.axis_index("tile")
    s = lax.axis_index("sub")
    fields = atm.shape[0]
    pairs = w_hbm.shape[0]
    width = w_hbm.shape[3]
    cols = width // CHUNKS
    layers = c_hbm.shape[0]
    blocks = owner.shape[1]
    slab = CAP_P * fields
    prows = pairs * SUBL
    nslot = 3 * subs * slab
    per_part = pairs // WPARTS
    padcap = val_s.shape[1]

    w_copies = []
    for c in range(CHUNKS):
        for g in range(WPARTS):
            part = pl.ds(g * per_part, per_part)
            copy = pltpu.make_async_copy(
                w_hbm.at[part, :, :, pl.ds(c * cols, cols)], w_v.at[c, part], w_sem.at[c, g]
            )
            copy.start()
            w_copies.append(copy)
    c_copy = pltpu.make_async_copy(c_hbm, c_raw, cm_sem.at[0])
    m_copy = pltpu.make_async_copy(m_hbm, m_raw, cm_sem.at[1])
    c_copy.start()
    m_copy.start()

    near = []
    for i in range(1, subs):
        near.append((1, lax.rem(s + i, subs)))
    for i in range(subs):
        for o in (0, 2):
            near.append((o, lax.rem(s + i, subs)))
    partners = [(lax.rem(t + o - 1 + tiles, tiles), ds) for o, ds in near]
    far = [lax.rem(t + i, tiles) for i in range(1, tiles)]
    everyone = partners + [(far[i - 1], s) for i in range(2, tiles - 1)]
    barrier = pltpu.get_barrier_semaphore()
    for who in everyone:
        pl.semaphore_signal(barrier, inc=1, device_id=who, device_id_type=MESH)
    edge_s[0, 0:fields, :] = atm[:, SUBL - 1, :]
    edge_s[1, 0:fields, :] = atm[:, 0, :]
    pl.semaphore_wait(barrier, len(everyone))

    me = t * subs + s
    total = tiles * subs
    edge_copies = []
    for k, to in enumerate((lax.rem(me + 1, total), lax.rem(me + total - 1, total))):
        copy = pltpu.make_async_remote_copy(
            src_ref=edge_s.at[k], dst_ref=edge_r.at[k], send_sem=edge_ss.at[k], recv_sem=edge_rs.at[k],
            device_id=(to // subs, lax.rem(to, subs)), device_id_type=MESH,
        )
        copy.start()
        edge_copies.append(copy)

    prow = iota((prows, pairs), 0) >> 3
    plane = iota((prows, pairs), 1)
    mine = prow == plane
    land = pair_land[...]
    device = land // LB_DEV
    offset = (device // subs - t + 1 + tiles) % tiles
    group = (offset * subs + device % subs).astype(f32)
    atm_row = pair_atm[...].astype(f32)
    local = (land % LB_DEV).astype(f32)

    def column(row):
        return jnp.sum(jnp.where(mine, row, 0.0), axis=1, keepdims=True)

    group_col = column(group)
    rank_col = jnp.sum(
        jnp.where((group == group_col) & (plane < prow), 1.0, 0.0), axis=1, keepdims=True
    )
    atm_col = column(atm_row).astype(i32)
    local_col = column(local)
    f_col = iota((prows, 1), 0) & 7
    real = f_col < fields
    group_i = group_col.astype(i32)
    rank_i = rank_col.astype(i32)
    slot_col = jnp.where(real, (group_i * CAP_P + rank_i) * fields + f_col, -1)
    a_t = jnp.where(iota((prows, nslot), 1) == slot_col, 1.0, 0.0)
    amat[...] = jnp.transpose(a_t).astype(bf16)
    ngroup = meta_s.shape[0]
    g_t = jnp.where(iota((prows, LANES), 1) == group_i, 1.0, 0.0)
    code = (f_col * LB_DEV).astype(f32) + local_col + 1.0
    q_t = jnp.where((iota((prows, LANES), 1) == rank_i * fields + f_col) & real, code, 0.0)
    metas = jnp.dot(
        jnp.transpose(g_t).astype(bf16), q_t.astype(bf16), preferred_element_type=f32
    )
    for g in range(ngroup):
        meta_s[g] = jnp.broadcast_to(metas[g : g + 1, :], (SUBL, LANES))
    own = subs + s

    def sends(src, dst, ssem, rsem):
        copies = []
        for (o, ds), who in zip(near, partners):
            copy = pltpu.make_async_remote_copy(
                src_ref=src.at[o * subs + ds], dst_ref=dst.at[o * subs + s],
                send_sem=ssem.at[o * subs + ds], recv_sem=rsem.at[o * subs + s],
                device_id=who, device_id_type=MESH,
            )
            copy.start()
            copies.append(copy)
        return copies

    def arrivals(src, dst, ssem, rsem):
        for (o, ds), who in zip(near, partners):
            pltpu.make_async_remote_copy(
                src_ref=src.at[o * subs + ds], dst_ref=dst.at[o * subs + ds],
                send_sem=ssem.at[o * subs + ds], recv_sem=rsem.at[o * subs + ds],
                device_id=who, device_id_type=MESH,
            ).wait_recv()

    meta_copies = sends(meta_s, meta_r, meta_ss, meta_rs)
    meta_r[pl.ds(own, 1)] = meta_s[pl.ds(own, 1)]

    for copy in edge_copies:
        copy.wait()
    cell = atm[...].reshape(fields * SUBL, LANES)
    lane = iota(cell.shape, 1)
    arow = iota(cell.shape, 0) & 7
    right = pltpu.roll(cell, LANES - 1, 1)
    left = pltpu.roll(cell, 1, 1)
    grad_x = jnp.where(
        lane == 0, right - cell, jnp.where(lane == LANES - 1, cell - left, (right - left) * 0.5)
    )
    before = jnp.concatenate(
        [jnp.broadcast_to(edge_r[0, f : f + 1, :], (SUBL, LANES)) for f in range(fields)], axis=0
    )
    after = jnp.concatenate(
        [jnp.broadcast_to(edge_r[1, f : f + 1, :], (SUBL, LANES)) for f in range(fields)], axis=0
    )
    down = jnp.where(arow == SUBL - 1, after, pltpu.roll(cell, fields * SUBL - 1, 0))
    up = jnp.where(arow == 0, before, pltpu.roll(cell, 1, 0))
    grad_y = (down - up) * 0.5
    stacked = jnp.concatenate([cell, grad_x, grad_y], axis=1).astype(bf16)
    pick = jnp.where(
        iota((prows, fields * SUBL), 1) == f_col * SUBL + atm_col, 1.0, 0.0
    ).astype(bf16)
    picked[...] = jnp.dot(pick, stacked, preferred_element_type=f32)

    slot_copies = []
    for c in range(CHUNKS):
        for g in range(WPARTS):
            w_copies[c * WPARTS + g].wait()
            for p in range(g * per_part, (g + 1) * per_part):
                rows = picked[p * SUBL : (p + 1) * SUBL, :].astype(bf16)
                pbuf[p * SUBL : (p + 1) * SUBL, :] = jnp.dot(
                    rows, w_v[c, p].reshape(3 * LANES, cols), preferred_element_type=f32
                )
        slots = split_dot(amat[...], pbuf[...])
        slot_s[c] = slots.reshape(3 * subs, slab, cols)
        slot_copies += sends(slot_s.at[c], slot_r.at[c], slot_ss.at[c], slot_rs.at[c])
        slot_r[c, pl.ds(own, 1)] = slot_s[c, pl.ds(own, 1)]

    k_row = iota((blocks, blocks), 0)
    natural = (k_row & (LB_DEV - 1)) * (blocks // LB_DEV) + k_row // LB_DEV
    j_lane = iota((blocks, blocks), 1)
    own_row = owner[...].astype(f32)
    own_col = jnp.sum(jnp.where(j_lane == natural, own_row, 0.0), axis=1, keepdims=True)
    river_rank = jnp.sum(
        jnp.where((own_row == own_col) & (j_lane < natural), 1.0, 0.0), axis=1, keepdims=True
    ).astype(i32)
    own_i = own_col.astype(i32)
    r_t = jnp.where(iota((blocks, tiles * padcap), 1) == own_i * padcap + river_rank, 1.0, 0.0)
    rmat[...] = jnp.transpose(r_t).astype(bf16)
    o_t = jnp.where(iota((blocks, LANES), 1) == own_i, 1.0, 0.0)
    n_t = jnp.where(
        iota((blocks, LANES), 1) == river_rank, natural[:, 0:1].astype(f32) + 1.0, 0.0
    )
    numbers = jnp.dot(
        jnp.transpose(o_t).astype(bf16), n_t.astype(bf16), preferred_element_type=f32
    )
    for to in range(tiles):
        num_s[to] = jnp.broadcast_to(numbers[to : to + 1, :], (SUBL, LANES))

    def river_sends(src, dst, ssem, rsem):
        copies = []
        for to in far:
            copy = pltpu.make_async_remote_copy(
                src_ref=src.at[to], dst_ref=dst.at[t], send_sem=ssem.at[to], recv_sem=rsem.at[t],
                device_id=(to, s), device_id_type=MESH,
            )
            copy.start()
            copies.append(copy)
        dst[pl.ds(t, 1)] = src[pl.ds(t, 1)]
        return copies

    def river_arrivals(src, dst, ssem, rsem):
        for to in far:
            pltpu.make_async_remote_copy(
                src_ref=src.at[to], dst_ref=dst.at[to], send_sem=ssem.at[to], recv_sem=rsem.at[to],
                device_id=(to, s), device_id_type=MESH,
            ).wait_recv()

    num_copies = river_sends(num_s, num_r, num_ss, num_rs)

    groups = width // LANES
    c_copy.wait()
    m_copy.wait()

    def place(q, half, b):
        return pl.ds((half * SUBL + b) * width + q * LANES, LANES)

    for raw, out in ((c_raw, ct), (m_raw, mt)):
        for q in range(groups):
            for half in range(LB_DEV // SUBL):
                for k0 in range(0, layers, SUBL):
                    n = min(SUBL, layers - k0)
                    regs = []
                    for b in range(SUBL):
                        part = raw[k0 : k0 + n, place(q, half, b)]
                        if n < SUBL:
                            part = jnp.concatenate(
                                [part, jnp.zeros((SUBL - n, LANES), f32)], axis=0
                            )
                        regs.append(part)
                    regs = swap8(regs)
                    r0 = q * LB_DEV + half * SUBL
                    for k in range(n):
                        out[k0 + k, r0 : r0 + SUBL, :] = regs[k]
    inverse = None
    for k in range(layers):
        diagonal = 1.0 + ct[k]
        if k > 0:
            before_c = ct[k - 1]
            diagonal = diagonal + before_c - before_c * before_c * inverse
        inverse = 1.0 / diagonal
        it[k] = inverse
        rt[k] = ct[k] * inverse
        if k > 0:
            gt[k] = before_c * inverse

    arrivals(meta_s, meta_r, meta_ss, meta_rs)
    spot = iota((slab, LANES), 0) == iota((slab, LANES), 1)
    for g in range(ngroup):
        row = jnp.broadcast_to(meta_r[g, 0:1, :], (slab, LANES))
        got = jnp.sum(jnp.where(spot, row, 0.0), axis=1, keepdims=True).astype(i32) - 1
        second = jnp.where(got < 0, -1, (got & (LB_DEV - 1)) * SUBL + (got >> 4))
        wide = iota((slab, LANES), 1)
        bmat[g * slab : (g + 1) * slab, 0:LANES] = jnp.where(wide == got, 1.0, 0.0)
        bmat[g * slab : (g + 1) * slab, LANES : 2 * LANES] = jnp.where(wide == second, 1.0, 0.0)
    b_all = jnp.transpose(bmat[...]).astype(bf16)

    half_rows = LB_DEV * cols // LANES
    for c in range(CHUNKS):
        arrivals(slot_s.at[c], slot_r.at[c], slot_ss.at[c], slot_rs.at[c])
        sums = split_dot(b_all, slot_r[c].reshape(nslot, cols))
        for b in range(LB_DEV):
            forcing_out[:, b * width + c * cols : b * width + (c + 1) * cols] = sums[
                LANES + b * SUBL : LANES + b * SUBL + fields, :
            ].astype(bf16)

        def field(f):
            part = sums[f * LB_DEV : (f + 1) * LB_DEV, :]
            return jnp.concatenate(
                [part[:, q * LANES : (q + 1) * LANES] for q in range(cols // LANES)], axis=0
            )

        wet = jnp.concatenate(
            [
                mask[pl.ds(c * (cols // LANES) + q, LB_DEV, stride=groups), :]
                for q in range(cols // LANES)
            ],
            axis=0,
        ).astype(f32)
        soft = softplus(field(0))
        share = sigmoid(field(1))
        source = wet * (soft * share - 0.5 * sigmoid(field(2)) * softplus(field(3)))
        surface = wet * soft * (1.0 - share)
        here = slice(c * half_rows, (c + 1) * half_rows)
        drainage = jnp.zeros_like(surface)
        for step in range(SOIL_STEPS):
            value = (mt[0, here, :] + source) * it[0, here, :]
            fwd[0] = value
            for k in range(1, layers):
                value = mt[k, here, :] * it[k, here, :] + gt[k, here, :] * value
                fwd[k] = value
            drainage = drainage + ct[layers - 1, here, :] * value
            mt[layers - 1, here, :] = value
            for k in range(layers - 2, -1, -1):
                value = fwd[k] + rt[k, here, :] * value
                mt[k, here, :] = value
        runoff[here, :] = wet * (SOIL_STEPS * surface + drainage)
        if c == CHUNKS - 1:
            values = split_dot(rmat[...], runoff[...])
            val_s[...] = values.reshape(tiles, padcap, LANES)
            val_copies = river_sends(val_s, val_r, val_ss, val_rs)
        for q in range(c * (cols // LANES), (c + 1) * (cols // LANES)):
            for half in range(LB_DEV // SUBL):
                r0 = q * LB_DEV + half * SUBL
                for k0 in range(0, layers, SUBL):
                    n = min(SUBL, layers - k0)
                    regs = [mt[k0 + min(k, n - 1), r0 : r0 + SUBL, :] for k in range(SUBL)]
                    regs = swap8(regs)
                    for b in range(SUBL):
                        soil_v[k0 : k0 + n, place(q, half, b)] = regs[b][:n, :]
    soil_copy = pltpu.make_async_copy(soil_v, soil_out, out_sem)
    soil_copy.start()

    river_arrivals(num_s, num_r, num_ss, num_rs)
    got = num_r[:, 0, :].astype(i32)[:, :capacity]
    base = (iota(got.shape, 0) * subs + s) * blocks
    number_out[...] = jnp.where(got > 0, got - 1 + base, -1)
    river_arrivals(val_s, val_r, val_ss, val_rs)
    river_out[...] = val_r[...]
    for copy in meta_copies + slot_copies + num_copies + val_copies:
        copy.wait_send()
    soil_copy.wait()


def on_device(
    tiles, subs, atm_fields, pair_atm, pair_land, pair_weight, land_mask, conductance, soil_moisture,
    river_owner,
):
    fields = atm_fields.shape[0]
    pairs = pair_atm.shape[0]
    layers, cells = conductance.shape
    blocks = river_owner.shape[0]
    width = pair_weight.shape[3]
    cols = width // CHUNKS
    capacity = max(2, 2 * blocks // tiles)
    padcap = -(-capacity // SUBL) * SUBL
    groups = 3 * subs
    slab = CAP_P * fields
    rows = cells // LANES
    dma = pltpu.SemaphoreType.DMA
    vmem = pl.BlockSpec(memory_space=pltpu.VMEM)
    anywhere = pl.BlockSpec(memory_space=pl.ANY)
    half_rows = rows // CHUNKS
    forcing, soil, values, numbers = pl.pallas_call(
        functools.partial(kernel, tiles, subs, capacity),
        out_shape=(
            jax.ShapeDtypeStruct((fields, cells), bf16),
            jax.ShapeDtypeStruct((layers, cells), f32),
            jax.ShapeDtypeStruct((tiles, padcap, LANES), f32),
            jax.ShapeDtypeStruct((tiles, capacity), i32),
        ),
        in_specs=[vmem] * 5 + [anywhere] * 3,
        out_specs=(vmem, anywhere, vmem, vmem),
        scratch_shapes=[
            pltpu.VMEM((CHUNKS, pairs, 3, LANES, cols), bf16),
            pltpu.VMEM((layers, cells), f32),
            pltpu.VMEM((layers, cells), f32),
            pltpu.VMEM((layers, rows, LANES), f32),
            pltpu.VMEM((layers, rows, LANES), f32),
            pltpu.VMEM((layers, rows, LANES), f32),
            pltpu.VMEM((layers, rows, LANES), f32),
            pltpu.VMEM((layers, rows, LANES), f32),
            pltpu.VMEM((layers, half_rows, LANES), f32),
            pltpu.VMEM((layers, cells), f32),
            pltpu.VMEM((2, SUBL, LANES), f32),
            pltpu.VMEM((2, SUBL, LANES), f32),
            pltpu.VMEM((groups, SUBL, LANES), f32),
            pltpu.VMEM((groups, SUBL, LANES), f32),
            pltpu.VMEM((CHUNKS, groups, slab, cols), f32),
            pltpu.VMEM((CHUNKS, groups, slab, cols), f32),
            pltpu.VMEM((tiles, SUBL, LANES), f32),
            pltpu.VMEM((tiles, SUBL, LANES), f32),
            pltpu.VMEM((tiles, padcap, LANES), f32),
            pltpu.VMEM((tiles, padcap, LANES), f32),
            pltpu.VMEM((pairs * SUBL, 3 * LANES), f32),
            pltpu.VMEM((pairs * SUBL, cols), f32),
            pltpu.VMEM((groups * slab, pairs * SUBL), bf16),
            pltpu.VMEM((groups * slab, 2 * LANES), f32),
            pltpu.VMEM((tiles * padcap, blocks), bf16),
            pltpu.VMEM((rows, LANES), f32),
            dma((CHUNKS, WPARTS)),
            dma((2,)),
            dma(()),
            dma((2,)),
            dma((2,)),
            dma((groups,)),
            dma((groups,)),
            dma((CHUNKS, groups)),
            dma((CHUNKS, groups)),
            dma((tiles,)),
            dma((tiles,)),
            dma((tiles,)),
            dma((tiles,)),
        ],
        compiler_params=pltpu.CompilerParams(
            collective_id=0, has_side_effects=True, vmem_limit_bytes=48 * 2**20
        ),
    )(
        atm_fields, pair_atm.reshape(1, pairs), pair_land.reshape(1, pairs),
        river_owner.reshape(1, blocks), land_mask.reshape(rows, LANES),
        pair_weight, conductance, soil_moisture,
    )
    return (forcing, soil, values[None, None, :, :capacity, :], numbers[None, None])


def solution(mesh):
    both = ("tile", "sub")
    return jax.shard_map(
        functools.partial(on_device, mesh.shape["tile"], mesh.shape["sub"]),
        mesh=mesh,
        in_specs=(
            P(None, both, None),
            P(both),
            P(both),
            P(both, None, None, None),
            P(both),
            P(None, both),
            P(None, both),
            P(both),
        ),
        out_specs=(
            P(None, both),
            P(None, both),
            P("tile", "sub", None, None, None),
            P("tile", "sub", None, None),
        ),
        check_vma=False,
    )
```

```python
import functools

import jax
import jax.numpy as jnp
from jax import lax
from jax.experimental import pallas as pl
from jax.experimental.pallas import tpu as pltpu
from jax.sharding import PartitionSpec as P

MESH = pl.DeviceIdType.MESH
SOIL_STEPS = 4
LB_DEV = 16
CAP_P = 4
LANES = 128
SUBL = 8
CHUNKS = 2
WPARTS = 4
f32 = jnp.float32
bf16 = jnp.bfloat16
i32 = jnp.int32


def iota(shape, dim):
    return lax.broadcasted_iota(i32, shape, dim)


def split_dot(onehot, values):
    high = values.astype(bf16)
    low = (values - high.astype(f32)).astype(bf16)
    return jnp.dot(onehot, high, preferred_element_type=f32) + jnp.dot(
        onehot, low, preferred_element_type=f32
    )


def swap8(regs):
    row = iota((SUBL, LANES), 0)
    regs = list(regs)
    for step in (1, 2, 4):
        keep = (row & step) == 0
        out = list(regs)
        for i in range(8):
            if i & step == 0:
                a, b = regs[i], regs[i + step]
                out[i] = jnp.where(keep, a, pltpu.roll(b, step, 0))
                out[i + step] = jnp.where(keep, pltpu.roll(a, SUBL - step, 0), b)
        regs = out
    return regs


def softplus(x):
    return jnp.maximum(x, 0.0) + jnp.log1p(jnp.exp(-jnp.abs(x)))


def sigmoid(x):
    return 1.0 / (1.0 + jnp.exp(-x))


def kernel(
    tiles, subs, capacity,
    atm_h, pair_atm_h, pair_land_h, owner_h, mask_h, w_hbm, c_hbm, m_hbm,
    forcing_h, soil_h, river_h, number_h,
    atm, pair_atm, pair_land, owner, mask, forcing_v, number_v,
    w_v, c_raw, m_raw, ct, mt, gt, rt, it, ut, fwd, soil_v, unit_v, edge_s, edge_r, meta_s, meta_r,
    slot_s, slot_r, num_s, num_r, val_s, val_r, pick_v, pbuf, amat, bmat, rmat, runoff, drain, drain_u,
    in_sem, w_sem, cm_sem, out_sem, edge_ss, edge_rs, meta_ss, meta_rs, slot_ss, slot_rs,
    num_ss, num_rs, val_ss, val_rs,
):
    t = lax.axis_index("tile")
    s = lax.axis_index("sub")
    fields = atm.shape[0]
    pairs = w_hbm.shape[0]
    width = w_hbm.shape[3]
    cols = width // CHUNKS
    layers = c_hbm.shape[0]
    blocks = owner.shape[1]
    slab = CAP_P * fields
    prows = pairs * SUBL
    nslot = 3 * subs * slab
    per_part = pairs // WPARTS
    padcap = val_s.shape[1]

    in_copies = []
    for k, (src, dst) in enumerate(
        ((atm_h, atm), (pair_atm_h, pair_atm), (pair_land_h, pair_land), (owner_h, owner), (mask_h, mask))
    ):
        copy = pltpu.make_async_copy(src, dst, in_sem.at[k])
        copy.start()
        in_copies.append(copy)
    w_copies = []
    for c in range(CHUNKS):
        for g in range(WPARTS):
            part = pl.ds(g * per_part, per_part)
            copy = pltpu.make_async_copy(
                w_hbm.at[part, :, :, pl.ds(c * cols, cols)], w_v.at[c, part], w_sem.at[c, g]
            )
            copy.start()
            w_copies.append(copy)
    c_copy = pltpu.make_async_copy(c_hbm, c_raw, cm_sem.at[0])
    m_copy = pltpu.make_async_copy(m_hbm, m_raw, cm_sem.at[1])
    c_copy.start()
    m_copy.start()

    near = []
    for i in range(subs):
        for o in (0, 2):
            near.append((o, lax.rem(s + i, subs)))
    for i in range(1, subs):
        near.append((1, lax.rem(s + i, subs)))
    partners = [(lax.rem(t + o - 1 + tiles, tiles), ds) for o, ds in near]
    far = [lax.rem(t + i, tiles) for i in range(1, tiles)]
    everyone = partners + [(far[i - 1], s) for i in range(2, tiles - 1)]
    barrier = pltpu.get_barrier_semaphore()
    for who in everyone:
        pl.semaphore_signal(barrier, inc=1, device_id=who, device_id_type=MESH)
    for copy in in_copies:
        copy.wait()
    edge_s[0, 0:fields, :] = atm[:, SUBL - 1, :]
    edge_s[1, 0:fields, :] = atm[:, 0, :]
    pl.semaphore_wait(barrier, len(everyone))

    me = t * subs + s
    total = tiles * subs
    edge_copies = []
    for k, to in enumerate((lax.rem(me + 1, total), lax.rem(me + total - 1, total))):
        copy = pltpu.make_async_remote_copy(
            src_ref=edge_s.at[k], dst_ref=edge_r.at[k], send_sem=edge_ss.at[k], recv_sem=edge_rs.at[k],
            device_id=(to // subs, lax.rem(to, subs)), device_id_type=MESH,
        )
        copy.start()
        edge_copies.append(copy)

    prow = iota((prows, pairs), 0) >> 3
    plane = iota((prows, pairs), 1)
    mine = prow == plane
    land = pair_land[...]
    device = land // LB_DEV
    offset = (device // subs - t + 1 + tiles) % tiles
    group = (offset * subs + device % subs).astype(f32)
    atm_row = pair_atm[...].astype(f32)
    local = (land % LB_DEV).astype(f32)

    def column(row):
        return jnp.sum(jnp.where(mine, row, 0.0), axis=1, keepdims=True)

    group_col = column(group)
    rank_col = jnp.sum(
        jnp.where((group == group_col) & (plane < prow), 1.0, 0.0), axis=1, keepdims=True
    )
    atm_col = column(atm_row).astype(i32)
    local_col = column(local)
    f_col = iota((prows, 1), 0) & 7
    real = f_col < fields
    group_i = group_col.astype(i32)
    rank_i = rank_col.astype(i32)
    slot_col = jnp.where(real, (group_i * CAP_P + rank_i) * fields + f_col, -1)
    a_t = jnp.where(iota((prows, nslot), 1) == slot_col, 1.0, 0.0)
    amat[...] = jnp.transpose(a_t).astype(bf16)
    ngroup = meta_s.shape[0]
    g_t = jnp.where(iota((prows, LANES), 1) == group_i, 1.0, 0.0)
    code = (f_col * LB_DEV).astype(f32) + local_col + 1.0
    q_t = jnp.where((iota((prows, LANES), 1) == rank_i * fields + f_col) & real, code, 0.0)
    metas = jnp.dot(
        jnp.transpose(g_t).astype(bf16), q_t.astype(bf16), preferred_element_type=f32
    )
    for g in range(ngroup):
        meta_s[g] = jnp.broadcast_to(metas[g : g + 1, :], (SUBL, LANES))
    own = subs + s

    def sends(src, dst, ssem, rsem):
        copies = []
        for (o, ds), who in zip(near, partners):
            copy = pltpu.make_async_remote_copy(
                src_ref=src.at[o * subs + ds], dst_ref=dst.at[o * subs + s],
                send_sem=ssem.at[o * subs + ds], recv_sem=rsem.at[o * subs + s],
                device_id=who, device_id_type=MESH,
            )
            copy.start()
            copies.append(copy)
        return copies

    def arrivals(src, dst, ssem, rsem):
        for (o, ds), who in zip(near, partners):
            pltpu.make_async_remote_copy(
                src_ref=src.at[o * subs + ds], dst_ref=dst.at[o * subs + ds],
                send_sem=ssem.at[o * subs + ds], recv_sem=rsem.at[o * subs + ds],
                device_id=who, device_id_type=MESH,
            ).wait_recv()

    meta_copies = sends(meta_s, meta_r, meta_ss, meta_rs)
    meta_r[pl.ds(own, 1)] = meta_s[pl.ds(own, 1)]

    cell = atm[...].reshape(fields * SUBL, LANES)
    lane = iota(cell.shape, 1)
    arow = iota(cell.shape, 0) & 7
    right = pltpu.roll(cell, LANES - 1, 1)
    left = pltpu.roll(cell, 1, 1)
    grad_x = jnp.where(
        lane == 0, right - cell, jnp.where(lane == LANES - 1, cell - left, (right - left) * 0.5)
    )
    pick = jnp.where(
        iota((prows, fields * SUBL), 1) == f_col * SUBL + atm_col, 1.0, 0.0
    ).astype(bf16)
    pick_v[:, 0 : 2 * LANES] = jnp.dot(
        pick, jnp.concatenate([cell, grad_x], axis=1).astype(bf16), preferred_element_type=f32
    )
    for c in range(CHUNKS):
        for g in range(WPARTS):
            w_copies[c * WPARTS + g].wait()
            for p in range(g * per_part, (g + 1) * per_part):
                rows = pick_v[p * SUBL : (p + 1) * SUBL, 0 : 2 * LANES].astype(bf16)
                pbuf[c, p * SUBL : (p + 1) * SUBL, :] = jnp.dot(
                    rows, w_v[c, p, 0:2].reshape(2 * LANES, cols), preferred_element_type=f32
                )

    for copy in edge_copies:
        copy.wait()
    before = jnp.concatenate(
        [jnp.broadcast_to(edge_r[0, f : f + 1, :], (SUBL, LANES)) for f in range(fields)], axis=0
    )
    after = jnp.concatenate(
        [jnp.broadcast_to(edge_r[1, f : f + 1, :], (SUBL, LANES)) for f in range(fields)], axis=0
    )
    down = jnp.where(arow == SUBL - 1, after, pltpu.roll(cell, fields * SUBL - 1, 0))
    up = jnp.where(arow == 0, before, pltpu.roll(cell, 1, 0))
    grad_y = (down - up) * 0.5
    pick_v[:, 2 * LANES :] = jnp.dot(pick, grad_y.astype(bf16), preferred_element_type=f32)

    slot_copies = []
    for c in range(CHUNKS):
        for p in range(pairs):
            rows = pick_v[p * SUBL : (p + 1) * SUBL, 2 * LANES :].astype(bf16)
            pbuf[c, p * SUBL : (p + 1) * SUBL, :] += jnp.dot(
                rows, w_v[c, p, 2], preferred_element_type=f32
            )
        slots = split_dot(amat[...], pbuf[c])
        slot_s[c] = slots.reshape(3 * subs, slab, cols)
        slot_copies += sends(slot_s.at[c], slot_r.at[c], slot_ss.at[c], slot_rs.at[c])
        slot_r[c, pl.ds(own, 1)] = slot_s[c, pl.ds(own, 1)]

    k_row = iota((blocks, blocks), 0)
    natural = (k_row & (LB_DEV - 1)) * (blocks // LB_DEV) + k_row // LB_DEV
    j_lane = iota((blocks, blocks), 1)
    own_row = owner[...].astype(f32)
    own_col = jnp.sum(jnp.where(j_lane == natural, own_row, 0.0), axis=1, keepdims=True)
    river_rank = jnp.sum(
        jnp.where((own_row == own_col) & (j_lane < natural), 1.0, 0.0), axis=1, keepdims=True
    ).astype(i32)
    own_i = own_col.astype(i32)
    r_t = jnp.where(iota((blocks, tiles * padcap), 1) == own_i * padcap + river_rank, 1.0, 0.0)
    rmat[...] = jnp.transpose(r_t).astype(bf16)
    o_t = jnp.where(iota((blocks, LANES), 1) == own_i, 1.0, 0.0)
    n_t = jnp.where(
        iota((blocks, LANES), 1) == river_rank, natural[:, 0:1].astype(f32) + 1.0, 0.0
    )
    numbers = jnp.dot(
        jnp.transpose(o_t).astype(bf16), n_t.astype(bf16), preferred_element_type=f32
    )
    for to in range(tiles):
        num_s[to] = jnp.broadcast_to(numbers[to : to + 1, :], (SUBL, LANES))

    def river_sends(src, dst, ssem, rsem):
        copies = []
        for to in far:
            copy = pltpu.make_async_remote_copy(
                src_ref=src.at[to], dst_ref=dst.at[t], send_sem=ssem.at[to], recv_sem=rsem.at[t],
                device_id=(to, s), device_id_type=MESH,
            )
            copy.start()
            copies.append(copy)
        dst[pl.ds(t, 1)] = src[pl.ds(t, 1)]
        return copies

    def river_arrivals(src, dst, ssem, rsem):
        for to in far:
            pltpu.make_async_remote_copy(
                src_ref=src.at[to], dst_ref=dst.at[to], send_sem=ssem.at[to], recv_sem=rsem.at[to],
                device_id=(to, s), device_id_type=MESH,
            ).wait_recv()

    num_copies = river_sends(num_s, num_r, num_ss, num_rs)

    groups = width // LANES
    c_copy.wait()
    m_copy.wait()

    def place(q, half, b):
        return pl.ds((half * SUBL + b) * width + q * LANES, LANES)

    for raw, out in ((c_raw, ct), (m_raw, mt)):
        for q in range(groups):
            for half in range(LB_DEV // SUBL):
                for k0 in range(0, layers, SUBL):
                    n = min(SUBL, layers - k0)
                    regs = []
                    for b in range(SUBL):
                        part = raw[k0 : k0 + n, place(q, half, b)]
                        if n < SUBL:
                            part = jnp.concatenate(
                                [part, jnp.zeros((SUBL - n, LANES), f32)], axis=0
                            )
                        regs.append(part)
                    regs = swap8(regs)
                    r0 = q * LB_DEV + half * SUBL
                    for k in range(n):
                        out[k0 + k, r0 : r0 + SUBL, :] = regs[k]
    inverse = None
    for k in range(layers):
        diagonal = 1.0 + ct[k]
        if k > 0:
            before_c = ct[k - 1]
            diagonal = diagonal + before_c - before_c * before_c * inverse
        inverse = 1.0 / diagonal
        it[k] = inverse
        rt[k] = ct[k] * inverse
        if k > 0:
            gt[k] = before_c * inverse

    arrivals(meta_s, meta_r, meta_ss, meta_rs)
    spot = iota((slab, LANES), 0) == iota((slab, LANES), 1)
    for g in range(ngroup):
        row = jnp.broadcast_to(meta_r[g, 0:1, :], (slab, LANES))
        got = jnp.sum(jnp.where(spot, row, 0.0), axis=1, keepdims=True).astype(i32) - 1
        second = jnp.where(got < 0, -1, (got & (LB_DEV - 1)) * SUBL + (got >> 4))
        wide = iota((slab, LANES), 1)
        bmat[g * slab : (g + 1) * slab, 0:LANES] = jnp.where(wide == got, 1.0, 0.0)
        bmat[g * slab : (g + 1) * slab, LANES : 2 * LANES] = jnp.where(wide == second, 1.0, 0.0)
    b_all = jnp.transpose(bmat[...]).astype(bf16)

    half_rows = LB_DEV * cols // LANES
    for c in range(CHUNKS):
        here = slice(c * half_rows, (c + 1) * half_rows)
        for step in range(SOIL_STEPS):
            plain = mt[0, here, :] * it[0, here, :]
            if step == 0:
                unit = it[0, here, :]
            else:
                unit = (ut[0, here, :] + 1.0) * it[0, here, :]
            fwd[0, 0] = plain
            fwd[1, 0] = unit
            for k in range(1, layers):
                g = gt[k, here, :]
                inv = it[k, here, :]
                plain = mt[k, here, :] * inv + g * plain
                unit = g * unit if step == 0 else ut[k, here, :] * inv + g * unit
                fwd[0, k] = plain
                fwd[1, k] = unit
            bottom = ct[layers - 1, here, :]
            if step == 0:
                drain[here, :] = bottom * plain
                drain_u[here, :] = bottom * unit
            else:
                drain[here, :] += bottom * plain
                drain_u[here, :] += bottom * unit
            mt[layers - 1, here, :] = plain
            ut[layers - 1, here, :] = unit
            for k in range(layers - 2, -1, -1):
                r = rt[k, here, :]
                plain = fwd[0, k] + r * plain
                unit = fwd[1, k] + r * unit
                mt[k, here, :] = plain
                ut[k, here, :] = unit
    for src, dst in ((mt, soil_v), (ut, unit_v)):
        for q in range(groups):
            for half in range(LB_DEV // SUBL):
                r0 = q * LB_DEV + half * SUBL
                for k0 in range(0, layers, SUBL):
                    n = min(SUBL, layers - k0)
                    regs = [src[k0 + min(k, n - 1), r0 : r0 + SUBL, :] for k in range(SUBL)]
                    regs = swap8(regs)
                    for b in range(SUBL):
                        dst[k0 : k0 + n, place(q, half, b)] = regs[b][:n, :]

    for c in range(CHUNKS):
        arrivals(slot_s.at[c], slot_r.at[c], slot_ss.at[c], slot_rs.at[c])
        sums = split_dot(b_all, slot_r[c].reshape(nslot, cols))

        def field(f):
            part = sums[f * LB_DEV : (f + 1) * LB_DEV, :]
            return jnp.concatenate(
                [part[:, q * LANES : (q + 1) * LANES] for q in range(cols // LANES)], axis=0
            )

        wet = jnp.concatenate(
            [
                mask[pl.ds(c * (cols // LANES) + q, LB_DEV, stride=groups), :]
                for q in range(cols // LANES)
            ],
            axis=0,
        ).astype(f32)
        soft = softplus(field(0))
        share = sigmoid(field(1))
        source = wet * (soft * share - 0.5 * sigmoid(field(2)) * softplus(field(3)))
        surface = wet * soft * (1.0 - share)
        here = slice(c * half_rows, (c + 1) * half_rows)
        drainage = drain[here, :] + source * drain_u[here, :]
        runoff[here, :] = wet * (SOIL_STEPS * surface + drainage)
        if c == CHUNKS - 1:
            values = split_dot(rmat[...], runoff[...])
            val_s[...] = values.reshape(tiles, padcap, LANES)
            val_copies = river_sends(val_s, val_r, val_ss, val_rs)
        for b in range(LB_DEV):
            forcing_v[:, b * width + c * cols : b * width + (c + 1) * cols] = sums[
                LANES + b * SUBL : LANES + b * SUBL + fields, :
            ].astype(bf16)
        for q in range(cols // LANES):
            for b in range(LB_DEV):
                at = place(c * (cols // LANES) + q, 0, b)
                row = source[q * LB_DEV + b : q * LB_DEV + b + 1, :]
                soil_v[:, at] += jnp.broadcast_to(row, (layers, LANES)) * unit_v[:, at]
    outs = [
        pltpu.make_async_copy(soil_v, soil_h, out_sem.at[0]),
        pltpu.make_async_copy(forcing_v, forcing_h, out_sem.at[1]),
    ]
    outs[0].start()
    outs[1].start()
    river_arrivals(num_s, num_r, num_ss, num_rs)
    got = num_r[:, 0, :].astype(i32)[:, :capacity]
    base = (iota(got.shape, 0) * subs + s) * blocks
    number_v[...] = jnp.where(got > 0, got - 1 + base, -1)
    outs.append(pltpu.make_async_copy(number_v, number_h, out_sem.at[2]))
    outs[2].start()
    for copy in meta_copies + slot_copies + num_copies:
        copy.wait_send()
    river_arrivals(val_s, val_r, val_ss, val_rs)
    outs.append(pltpu.make_async_copy(val_r, river_h, out_sem.at[3]))
    outs[3].start()
    for copy in val_copies:
        copy.wait_send()
    for copy in outs:
        copy.wait()


def hand_on(*refs):
    count = (len(refs) - 1) // 2
    sem = refs[-1]
    copies = []
    for k in range(count):
        copies.append(pltpu.make_async_copy(refs[k], refs[count + k], sem.at[k]))
        copies[-1].start()
    for copy in copies:
        copy.wait()


def on_device(
    tiles, subs, atm_fields, pair_atm, pair_land, pair_weight, land_mask, conductance, soil_moisture,
    river_owner,
):
    fields = atm_fields.shape[0]
    pairs = pair_atm.shape[0]
    layers, cells = conductance.shape
    blocks = river_owner.shape[0]
    width = pair_weight.shape[3]
    cols = width // CHUNKS
    capacity = max(2, 2 * blocks // tiles)
    padcap = -(-capacity // SUBL) * SUBL
    groups = 3 * subs
    slab = CAP_P * fields
    rows = cells // LANES
    dma = pltpu.SemaphoreType.DMA
    hbm = pl.BlockSpec(memory_space=pltpu.HBM)
    half_rows = rows // CHUNKS
    shapes = (
        jax.ShapeDtypeStruct((fields, cells), bf16),
        jax.ShapeDtypeStruct((layers, cells), f32),
        jax.ShapeDtypeStruct((tiles, padcap, LANES), f32),
        jax.ShapeDtypeStruct((tiles, capacity), i32),
    )
    column = pltpu.VMEM((layers, rows, LANES), f32)
    results = pl.pallas_call(
        functools.partial(kernel, tiles, subs, capacity),
        out_shape=shapes,
        in_specs=[hbm] * 8,
        out_specs=(hbm,) * 4,
        scratch_shapes=[
            pltpu.VMEM(atm_fields.shape, f32),
            pltpu.VMEM((1, pairs), i32),
            pltpu.VMEM((1, pairs), i32),
            pltpu.VMEM((1, blocks), i32),
            pltpu.VMEM((rows, LANES), i32),
            pltpu.VMEM((fields, cells), bf16),
            pltpu.VMEM((tiles, capacity), i32),
            pltpu.VMEM((CHUNKS, pairs, 3, LANES, cols), bf16),
            pltpu.VMEM((layers, cells), f32),
            pltpu.VMEM((layers, cells), f32),
            column,
            column,
            column,
            column,
            column,
            column,
            pltpu.VMEM((2, layers, half_rows, LANES), f32),
            pltpu.VMEM((layers, cells), f32),
            pltpu.VMEM((layers, cells), f32),
            pltpu.VMEM((2, SUBL, LANES), f32),
            pltpu.VMEM((2, SUBL, LANES), f32),
            pltpu.VMEM((groups, SUBL, LANES), f32),
            pltpu.VMEM((groups, SUBL, LANES), f32),
            pltpu.VMEM((CHUNKS, groups, slab, cols), f32),
            pltpu.VMEM((CHUNKS, groups, slab, cols), f32),
            pltpu.VMEM((tiles, SUBL, LANES), f32),
            pltpu.VMEM((tiles, SUBL, LANES), f32),
            pltpu.VMEM((tiles, padcap, LANES), f32),
            pltpu.VMEM((tiles, padcap, LANES), f32),
            pltpu.VMEM((pairs * SUBL, 3 * LANES), f32),
            pltpu.VMEM((CHUNKS, pairs * SUBL, cols), f32),
            pltpu.VMEM((groups * slab, pairs * SUBL), bf16),
            pltpu.VMEM((groups * slab, 2 * LANES), f32),
            pltpu.VMEM((tiles * padcap, blocks), bf16),
            pltpu.VMEM((rows, LANES), f32),
            pltpu.VMEM((rows, LANES), f32),
            pltpu.VMEM((rows, LANES), f32),
            dma((5,)),
            dma((CHUNKS, WPARTS)),
            dma((2,)),
            dma((4,)),
            dma((2,)),
            dma((2,)),
            dma((groups,)),
            dma((groups,)),
            dma((CHUNKS, groups)),
            dma((CHUNKS, groups)),
            dma((tiles,)),
            dma((tiles,)),
            dma((tiles,)),
            dma((tiles,)),
        ],
        compiler_params=pltpu.CompilerParams(
            collective_id=0, has_side_effects=True, vmem_limit_bytes=64 * 2**20
        ),
    )(
        atm_fields, pair_atm.reshape(1, pairs), pair_land.reshape(1, pairs),
        river_owner.reshape(1, blocks), land_mask.reshape(rows, LANES),
        pair_weight, conductance, soil_moisture,
    )
    forcing, soil, values, numbers = pl.pallas_call(
        hand_on,
        out_shape=shapes,
        in_specs=[hbm] * 4,
        out_specs=(hbm,) * 4,
        scratch_shapes=[dma((4,))],
        compiler_params=pltpu.CompilerParams(vmem_limit_bytes=64 * 2**20),
    )(*results)
    return (forcing, soil, values[None, None, :, :capacity, :], numbers[None, None])


def solution(mesh):
    both = ("tile", "sub")
    return jax.shard_map(
        functools.partial(on_device, mesh.shape["tile"], mesh.shape["sub"]),
        mesh=mesh,
        in_specs=(
            P(None, both, None),
            P(both),
            P(both),
            P(both, None, None, None),
            P(both),
            P(None, both),
            P(None, both),
            P(both),
        ),
        out_specs=(
            P(None, both),
            P(None, both),
            P("tile", "sub", None, None, None),
            P("tile", "sub", None, None),
        ),
        check_vma=False,
    )
```

```python
import functools

import jax
import jax.numpy as jnp
from jax import lax
from jax.experimental import pallas as pl
from jax.experimental.pallas import tpu as pltpu
from jax.sharding import PartitionSpec as P

MESH = pl.DeviceIdType.MESH
SOIL_STEPS = 4
LB_DEV = 16
CAP_P = 4
LANES = 128
SUBL = 8
CHUNKS = 2
WPARTS = 4
f32 = jnp.float32
bf16 = jnp.bfloat16
i32 = jnp.int32


def iota(shape, dim):
    return lax.broadcasted_iota(i32, shape, dim)


def split_dot(onehot, values):
    high = values.astype(bf16)
    low = (values - high.astype(f32)).astype(bf16)
    return jnp.dot(onehot, high, preferred_element_type=f32) + jnp.dot(
        onehot, low, preferred_element_type=f32
    )


def swap8(regs):
    row = iota((SUBL, LANES), 0)
    regs = list(regs)
    for step in (1, 2, 4):
        keep = (row & step) == 0
        out = list(regs)
        for i in range(8):
            if i & step == 0:
                a, b = regs[i], regs[i + step]
                out[i] = jnp.where(keep, a, pltpu.roll(b, step, 0))
                out[i + step] = jnp.where(keep, pltpu.roll(a, SUBL - step, 0), b)
        regs = out
    return regs


def softplus(x):
    return jnp.maximum(x, 0.0) + jnp.log1p(jnp.exp(-jnp.abs(x)))


def sigmoid(x):
    return 1.0 / (1.0 + jnp.exp(-x))


def kernel(
    tiles, subs, capacity,
    atm_h, pair_atm_h, pair_land_h, owner_h, mask_h, w_hbm, c_hbm, m_hbm,
    forcing_v, soil_v, river_v, number_v,
    atm, pair_atm, pair_land, owner, mask,
    w_v, c_raw, m_raw, ct, mt, gt, rt, it, ut, fwd, unit_v, edge_s, edge_r, meta_s, meta_r,
    slot_s, slot_r, num_s, num_r, val_s, val_r, pick_v, pbuf, amat, bmat, rmat, runoff, drain, drain_u,
    in_sem, w_sem, cm_sem, edge_ss, edge_rs, meta_ss, meta_rs, slot_ss, slot_rs,
    num_ss, num_rs, val_ss, val_rs,
):
    t = lax.axis_index("tile")
    s = lax.axis_index("sub")
    fields = atm.shape[0]
    pairs = w_hbm.shape[0]
    width = w_hbm.shape[3]
    cols = width // CHUNKS
    layers = c_hbm.shape[0]
    blocks = owner.shape[1]
    slab = CAP_P * fields
    prows = pairs * SUBL
    nslot = 3 * subs * slab
    per_part = pairs // WPARTS
    padcap = val_s.shape[1]

    near = []
    for i in range(subs):
        for o in (0, 2):
            near.append((o, lax.rem(s + i, subs)))
    for i in range(1, subs):
        near.append((1, lax.rem(s + i, subs)))
    partners = [(lax.rem(t + o - 1 + tiles, tiles), ds) for o, ds in near]
    far = [lax.rem(t + i, tiles) for i in range(1, tiles)]
    everyone = partners + [(far[i - 1], s) for i in range(2, tiles - 1)]
    barrier = pltpu.get_barrier_semaphore()
    for who in everyone:
        pl.semaphore_signal(barrier, inc=1, device_id=who, device_id_type=MESH)
    in_copies = []
    for k, (src, dst) in enumerate(
        ((atm_h, atm), (pair_atm_h, pair_atm), (pair_land_h, pair_land), (owner_h, owner), (mask_h, mask))
    ):
        copy = pltpu.make_async_copy(src, dst, in_sem.at[k])
        copy.start()
        in_copies.append(copy)
    w_copies = []
    for c in range(CHUNKS):
        for g in range(WPARTS):
            part = pl.ds(g * per_part, per_part)
            copy = pltpu.make_async_copy(
                w_hbm.at[part, :, :, pl.ds(c * cols, cols)], w_v.at[c, part], w_sem.at[c, g]
            )
            copy.start()
            w_copies.append(copy)
    c_copy = pltpu.make_async_copy(c_hbm, c_raw, cm_sem.at[0])
    m_copy = pltpu.make_async_copy(m_hbm, m_raw, cm_sem.at[1])
    c_copy.start()
    m_copy.start()

    for copy in in_copies:
        copy.wait()
    edge_s[0, 0:fields, :] = atm[:, SUBL - 1, :]
    edge_s[1, 0:fields, :] = atm[:, 0, :]
    pl.semaphore_wait(barrier, len(everyone))

    me = t * subs + s
    total = tiles * subs
    edge_copies = []
    for k, to in enumerate((lax.rem(me + 1, total), lax.rem(me + total - 1, total))):
        copy = pltpu.make_async_remote_copy(
            src_ref=edge_s.at[k], dst_ref=edge_r.at[k], send_sem=edge_ss.at[k], recv_sem=edge_rs.at[k],
            device_id=(to // subs, lax.rem(to, subs)), device_id_type=MESH,
        )
        copy.start()
        edge_copies.append(copy)

    prow = iota((prows, pairs), 0) >> 3
    plane = iota((prows, pairs), 1)
    mine = prow == plane
    land = pair_land[...]
    device = land // LB_DEV
    offset = (device // subs - t + 1 + tiles) % tiles
    group = (offset * subs + device % subs).astype(f32)
    atm_row = pair_atm[...].astype(f32)
    local = (land % LB_DEV).astype(f32)

    def column(row):
        return jnp.sum(jnp.where(mine, row, 0.0), axis=1, keepdims=True)

    group_col = column(group)
    rank_col = jnp.sum(
        jnp.where((group == group_col) & (plane < prow), 1.0, 0.0), axis=1, keepdims=True
    )
    atm_col = column(atm_row).astype(i32)
    local_col = column(local)
    f_col = iota((prows, 1), 0) & 7
    real = f_col < fields
    group_i = group_col.astype(i32)
    rank_i = rank_col.astype(i32)
    slot_col = jnp.where(real, (group_i * CAP_P + rank_i) * fields + f_col, -1)
    a_t = jnp.where(iota((prows, nslot), 1) == slot_col, 1.0, 0.0)
    amat[...] = jnp.transpose(a_t).astype(bf16)
    ngroup = meta_s.shape[0]
    g_t = jnp.where(iota((prows, LANES), 1) == group_i, 1.0, 0.0)
    code = (f_col * LB_DEV).astype(f32) + local_col + 1.0
    q_t = jnp.where((iota((prows, LANES), 1) == rank_i * fields + f_col) & real, code, 0.0)
    metas = jnp.dot(
        jnp.transpose(g_t).astype(bf16), q_t.astype(bf16), preferred_element_type=f32
    )
    for g in range(ngroup):
        meta_s[g] = jnp.broadcast_to(metas[g : g + 1, :], (SUBL, LANES))
    own = subs + s

    def sends(src, dst, ssem, rsem):
        copies = []
        for (o, ds), who in zip(near, partners):
            copy = pltpu.make_async_remote_copy(
                src_ref=src.at[o * subs + ds], dst_ref=dst.at[o * subs + s],
                send_sem=ssem.at[o * subs + ds], recv_sem=rsem.at[o * subs + s],
                device_id=who, device_id_type=MESH,
            )
            copy.start()
            copies.append(copy)
        return copies

    def arrivals(src, dst, ssem, rsem):
        for (o, ds), who in zip(near, partners):
            pltpu.make_async_remote_copy(
                src_ref=src.at[o * subs + ds], dst_ref=dst.at[o * subs + ds],
                send_sem=ssem.at[o * subs + ds], recv_sem=rsem.at[o * subs + ds],
                device_id=who, device_id_type=MESH,
            ).wait_recv()

    meta_copies = sends(meta_s, meta_r, meta_ss, meta_rs)
    meta_r[pl.ds(own, 1)] = meta_s[pl.ds(own, 1)]

    cell = atm[...].reshape(fields * SUBL, LANES)
    lane = iota(cell.shape, 1)
    arow = iota(cell.shape, 0) & 7
    right = pltpu.roll(cell, LANES - 1, 1)
    left = pltpu.roll(cell, 1, 1)
    grad_x = jnp.where(
        lane == 0, right - cell, jnp.where(lane == LANES - 1, cell - left, (right - left) * 0.5)
    )
    pick = jnp.where(
        iota((prows, fields * SUBL), 1) == f_col * SUBL + atm_col, 1.0, 0.0
    ).astype(bf16)
    pick_v[:, 0 : 2 * LANES] = jnp.dot(
        pick, jnp.concatenate([cell, grad_x], axis=1).astype(bf16), preferred_element_type=f32
    )
    def first_products(c):
        for g in range(WPARTS):
            w_copies[c * WPARTS + g].wait()
            for p in range(g * per_part, (g + 1) * per_part):
                rows = pick_v[p * SUBL : (p + 1) * SUBL, 0 : 2 * LANES].astype(bf16)
                pbuf[c, p * SUBL : (p + 1) * SUBL, :] = jnp.dot(
                    rows, w_v[c, p, 0:2].reshape(2 * LANES, cols), preferred_element_type=f32
                )

    first_products(0)
    for copy in edge_copies:
        copy.wait()
    before = jnp.concatenate(
        [jnp.broadcast_to(edge_r[0, f : f + 1, :], (SUBL, LANES)) for f in range(fields)], axis=0
    )
    after = jnp.concatenate(
        [jnp.broadcast_to(edge_r[1, f : f + 1, :], (SUBL, LANES)) for f in range(fields)], axis=0
    )
    down = jnp.where(arow == SUBL - 1, after, pltpu.roll(cell, fields * SUBL - 1, 0))
    up = jnp.where(arow == 0, before, pltpu.roll(cell, 1, 0))
    grad_y = (down - up) * 0.5
    pick_v[:, 2 * LANES :] = jnp.dot(pick, grad_y.astype(bf16), preferred_element_type=f32)

    slot_copies = []
    for c in range(CHUNKS):
        if c > 0:
            first_products(c)
        for p in range(pairs):
            rows = pick_v[p * SUBL : (p + 1) * SUBL, 2 * LANES :].astype(bf16)
            pbuf[c, p * SUBL : (p + 1) * SUBL, :] += jnp.dot(
                rows, w_v[c, p, 2], preferred_element_type=f32
            )
        slots = split_dot(amat[...], pbuf[c])
        slot_s[c] = slots.reshape(3 * subs, slab, cols)
        slot_copies += sends(slot_s.at[c], slot_r.at[c], slot_ss.at[c], slot_rs.at[c])
        slot_r[c, pl.ds(own, 1)] = slot_s[c, pl.ds(own, 1)]

    k_row = iota((blocks, blocks), 0)
    natural = (k_row & (LB_DEV - 1)) * (blocks // LB_DEV) + k_row // LB_DEV
    j_lane = iota((blocks, blocks), 1)
    own_row = owner[...].astype(f32)
    own_col = jnp.sum(jnp.where(j_lane == natural, own_row, 0.0), axis=1, keepdims=True)
    river_rank = jnp.sum(
        jnp.where((own_row == own_col) & (j_lane < natural), 1.0, 0.0), axis=1, keepdims=True
    ).astype(i32)
    own_i = own_col.astype(i32)
    r_t = jnp.where(iota((blocks, tiles * padcap), 1) == own_i * padcap + river_rank, 1.0, 0.0)
    rmat[...] = jnp.transpose(r_t).astype(bf16)
    o_t = jnp.where(iota((blocks, LANES), 1) == own_i, 1.0, 0.0)
    n_t = jnp.where(
        iota((blocks, LANES), 1) == river_rank, natural[:, 0:1].astype(f32) + 1.0, 0.0
    )
    numbers = jnp.dot(
        jnp.transpose(o_t).astype(bf16), n_t.astype(bf16), preferred_element_type=f32
    )
    for to in range(tiles):
        num_s[to] = jnp.broadcast_to(numbers[to : to + 1, :], (SUBL, LANES))

    def river_sends(src, dst, ssem, rsem):
        copies = []
        for to in far:
            copy = pltpu.make_async_remote_copy(
                src_ref=src.at[to], dst_ref=dst.at[t], send_sem=ssem.at[to], recv_sem=rsem.at[t],
                device_id=(to, s), device_id_type=MESH,
            )
            copy.start()
            copies.append(copy)
        dst[pl.ds(t, 1)] = src[pl.ds(t, 1)]
        return copies

    def river_arrivals(src, dst, ssem, rsem):
        for to in far:
            pltpu.make_async_remote_copy(
                src_ref=src.at[to], dst_ref=dst.at[to], send_sem=ssem.at[to], recv_sem=rsem.at[to],
                device_id=(to, s), device_id_type=MESH,
            ).wait_recv()

    num_copies = river_sends(num_s, num_r, num_ss, num_rs)

    groups = width // LANES
    c_copy.wait()
    m_copy.wait()

    def place(q, half, b):
        return pl.ds((half * SUBL + b) * width + q * LANES, LANES)

    for raw, out in ((c_raw, ct), (m_raw, mt)):
        for q in range(groups):
            for half in range(LB_DEV // SUBL):
                for k0 in range(0, layers, SUBL):
                    n = min(SUBL, layers - k0)
                    regs = []
                    for b in range(SUBL):
                        part = raw[k0 : k0 + n, place(q, half, b)]
                        if n < SUBL:
                            part = jnp.concatenate(
                                [part, jnp.zeros((SUBL - n, LANES), f32)], axis=0
                            )
                        regs.append(part)
                    regs = swap8(regs)
                    r0 = q * LB_DEV + half * SUBL
                    for k in range(n):
                        out[k0 + k, r0 : r0 + SUBL, :] = regs[k]
    inverse = None
    for k in range(layers):
        diagonal = 1.0 + ct[k]
        if k > 0:
            before_c = ct[k - 1]
            diagonal = diagonal + before_c - before_c * before_c * inverse
        inverse = 1.0 / diagonal
        it[k] = inverse
        rt[k] = ct[k] * inverse
        if k > 0:
            gt[k] = before_c * inverse

    arrivals(meta_s, meta_r, meta_ss, meta_rs)
    spot = iota((slab, LANES), 0) == iota((slab, LANES), 1)
    for g in range(ngroup):
        row = jnp.broadcast_to(meta_r[g, 0:1, :], (slab, LANES))
        got = jnp.sum(jnp.where(spot, row, 0.0), axis=1, keepdims=True).astype(i32) - 1
        second = jnp.where(got < 0, -1, (got & (LB_DEV - 1)) * SUBL + (got >> 4))
        wide = iota((slab, LANES), 1)
        bmat[g * slab : (g + 1) * slab, 0:LANES] = jnp.where(wide == got, 1.0, 0.0)
        bmat[g * slab : (g + 1) * slab, LANES : 2 * LANES] = jnp.where(wide == second, 1.0, 0.0)
    b_all = jnp.transpose(bmat[...]).astype(bf16)

    half_rows = LB_DEV * cols // LANES
    for c in range(CHUNKS):
        here = slice(c * half_rows, (c + 1) * half_rows)
        for step in range(SOIL_STEPS):
            plain = mt[0, here, :] * it[0, here, :]
            if step == 0:
                unit = it[0, here, :]
            else:
                unit = (ut[0, here, :] + 1.0) * it[0, here, :]
            fwd[0, 0] = plain
            fwd[1, 0] = unit
            for k in range(1, layers):
                g = gt[k, here, :]
                inv = it[k, here, :]
                plain = mt[k, here, :] * inv + g * plain
                unit = g * unit if step == 0 else ut[k, here, :] * inv + g * unit
                fwd[0, k] = plain
                fwd[1, k] = unit
            bottom = ct[layers - 1, here, :]
            if step == 0:
                drain[here, :] = bottom * plain
                drain_u[here, :] = bottom * unit
            else:
                drain[here, :] += bottom * plain
                drain_u[here, :] += bottom * unit
            mt[layers - 1, here, :] = plain
            ut[layers - 1, here, :] = unit
            for k in range(layers - 2, -1, -1):
                r = rt[k, here, :]
                plain = fwd[0, k] + r * plain
                unit = fwd[1, k] + r * unit
                mt[k, here, :] = plain
                ut[k, here, :] = unit
    for src, dst in ((mt, soil_v), (ut, unit_v)):
        for q in range(groups):
            for half in range(LB_DEV // SUBL):
                r0 = q * LB_DEV + half * SUBL
                for k0 in range(0, layers, SUBL):
                    n = min(SUBL, layers - k0)
                    regs = [src[k0 + min(k, n - 1), r0 : r0 + SUBL, :] for k in range(SUBL)]
                    regs = swap8(regs)
                    for b in range(SUBL):
                        dst[k0 : k0 + n, place(q, half, b)] = regs[b][:n, :]

    for c in range(CHUNKS):
        arrivals(slot_s.at[c], slot_r.at[c], slot_ss.at[c], slot_rs.at[c])
        sums = split_dot(b_all, slot_r[c].reshape(nslot, cols))

        def field(f):
            part = sums[f * LB_DEV : (f + 1) * LB_DEV, :]
            return jnp.concatenate(
                [part[:, q * LANES : (q + 1) * LANES] for q in range(cols // LANES)], axis=0
            )

        wet = jnp.concatenate(
            [
                mask[pl.ds(c * (cols // LANES) + q, LB_DEV, stride=groups), :]
                for q in range(cols // LANES)
            ],
            axis=0,
        ).astype(f32)
        soft = softplus(field(0))
        share = sigmoid(field(1))
        source = wet * (soft * share - 0.5 * sigmoid(field(2)) * softplus(field(3)))
        surface = wet * soft * (1.0 - share)
        here = slice(c * half_rows, (c + 1) * half_rows)
        drainage = drain[here, :] + source * drain_u[here, :]
        runoff[here, :] = wet * (SOIL_STEPS * surface + drainage)
        if c == CHUNKS - 1:
            values = split_dot(rmat[...], runoff[...])
            val_s[...] = values.reshape(tiles, padcap, LANES)
            val_copies = river_sends(val_s, val_r, val_ss, val_rs)
        for b in range(LB_DEV):
            forcing_v[:, b * width + c * cols : b * width + (c + 1) * cols] = sums[
                LANES + b * SUBL : LANES + b * SUBL + fields, :
            ].astype(bf16)
        for q in range(cols // LANES):
            for b in range(LB_DEV):
                at = place(c * (cols // LANES) + q, 0, b)
                row = source[q * LB_DEV + b : q * LB_DEV + b + 1, :]
                soil_v[:, at] += jnp.broadcast_to(row, (layers, LANES)) * unit_v[:, at]
    river_arrivals(num_s, num_r, num_ss, num_rs)
    got = num_r[:, 0, :].astype(i32)[:, :capacity]
    base = (iota(got.shape, 0) * subs + s) * blocks
    number_v[...] = jnp.where(got > 0, got - 1 + base, -1)
    for copy in meta_copies + slot_copies + num_copies:
        copy.wait_send()
    river_arrivals(val_s, val_r, val_ss, val_rs)
    river_v[...] = val_r[...]
    for copy in val_copies:
        copy.wait_send()


def hand_on(*refs):
    count = (len(refs) - 1) // 2
    sem = refs[-1]
    copies = []
    for k in range(count):
        copies.append(pltpu.make_async_copy(refs[k], refs[count + k], sem.at[k]))
        copies[-1].start()
    for copy in copies:
        copy.wait()


def on_device(
    tiles, subs, atm_fields, pair_atm, pair_land, pair_weight, land_mask, conductance, soil_moisture,
    river_owner,
):
    fields = atm_fields.shape[0]
    pairs = pair_atm.shape[0]
    layers, cells = conductance.shape
    blocks = river_owner.shape[0]
    width = pair_weight.shape[3]
    cols = width // CHUNKS
    capacity = max(2, 2 * blocks // tiles)
    padcap = -(-capacity // SUBL) * SUBL
    groups = 3 * subs
    slab = CAP_P * fields
    rows = cells // LANES
    dma = pltpu.SemaphoreType.DMA
    hbm = pl.BlockSpec(memory_space=pltpu.HBM)
    inside = pl.BlockSpec(memory_space=pltpu.VMEM)
    half_rows = rows // CHUNKS
    shapes = (
        ((fields, cells), bf16),
        ((layers, cells), f32),
        ((tiles, padcap, LANES), f32),
        ((tiles, capacity), i32),
    )
    column = pltpu.VMEM((layers, rows, LANES), f32)
    results = pl.pallas_call(
        functools.partial(kernel, tiles, subs, capacity),
        out_shape=[pltpu.VMEM(*shape) for shape in shapes],
        in_specs=[hbm] * 8,
        out_specs=[inside] * 4,
        scratch_shapes=[
            pltpu.VMEM(atm_fields.shape, f32),
            pltpu.VMEM((1, pairs), i32),
            pltpu.VMEM((1, pairs), i32),
            pltpu.VMEM((1, blocks), i32),
            pltpu.VMEM((rows, LANES), i32),
            pltpu.VMEM((CHUNKS, pairs, 3, LANES, cols), bf16),
            pltpu.VMEM((layers, cells), f32),
            pltpu.VMEM((layers, cells), f32),
            column,
            column,
            column,
            column,
            column,
            column,
            pltpu.VMEM((2, layers, half_rows, LANES), f32),
            pltpu.VMEM((layers, cells), f32),
            pltpu.VMEM((2, SUBL, LANES), f32),
            pltpu.VMEM((2, SUBL, LANES), f32),
            pltpu.VMEM((groups, SUBL, LANES), f32),
            pltpu.VMEM((groups, SUBL, LANES), f32),
            pltpu.VMEM((CHUNKS, groups, slab, cols), f32),
            pltpu.VMEM((CHUNKS, groups, slab, cols), f32),
            pltpu.VMEM((tiles, SUBL, LANES), f32),
            pltpu.VMEM((tiles, SUBL, LANES), f32),
            pltpu.VMEM((tiles, padcap, LANES), f32),
            pltpu.VMEM((tiles, padcap, LANES), f32),
            pltpu.VMEM((pairs * SUBL, 3 * LANES), f32),
            pltpu.VMEM((CHUNKS, pairs * SUBL, cols), f32),
            pltpu.VMEM((groups * slab, pairs * SUBL), bf16),
            pltpu.VMEM((groups * slab, 2 * LANES), f32),
            pltpu.VMEM((tiles * padcap, blocks), bf16),
            pltpu.VMEM((rows, LANES), f32),
            pltpu.VMEM((rows, LANES), f32),
            pltpu.VMEM((rows, LANES), f32),
            dma((5,)),
            dma((CHUNKS, WPARTS)),
            dma((2,)),
            dma((2,)),
            dma((2,)),
            dma((groups,)),
            dma((groups,)),
            dma((CHUNKS, groups)),
            dma((CHUNKS, groups)),
            dma((tiles,)),
            dma((tiles,)),
            dma((tiles,)),
            dma((tiles,)),
        ],
        compiler_params=pltpu.CompilerParams(
            collective_id=0, has_side_effects=True, vmem_limit_bytes=48 * 2**20
        ),
    )(
        *(
            pltpu.with_memory_space_constraint(array, pltpu.HBM)
            for array in (
                atm_fields, pair_atm.reshape(1, pairs), pair_land.reshape(1, pairs),
                river_owner.reshape(1, blocks), land_mask.reshape(rows, LANES),
                pair_weight, conductance, soil_moisture,
            )
        )
    )
    forcing, soil, values, numbers = pl.pallas_call(
        hand_on,
        out_shape=[jax.ShapeDtypeStruct(*shape) for shape in shapes],
        in_specs=[pl.BlockSpec(memory_space=pl.ANY)] * 4,
        out_specs=[hbm] * 4,
        scratch_shapes=[dma((4,))],
        compiler_params=pltpu.CompilerParams(vmem_limit_bytes=16 * 2**20),
    )(*(pltpu.with_memory_space_constraint(array, pltpu.VMEM) for array in results))
    return (forcing, soil, values[None, None, :, :capacity, :], numbers[None, None])


def solution(mesh):
    both = ("tile", "sub")
    return jax.shard_map(
        functools.partial(on_device, mesh.shape["tile"], mesh.shape["sub"]),
        mesh=mesh,
        in_specs=(
            P(None, both, None),
            P(both),
            P(both),
            P(both, None, None, None),
            P(both),
            P(None, both),
            P(None, both),
            P(both),
        ),
        out_specs=(
            P(None, both),
            P(None, both),
            P("tile", "sub", None, None, None),
            P("tile", "sub", None, None),
        ),
        check_vma=False,
    )
```

```python
import functools

import jax
import jax.numpy as jnp
from jax import lax
from jax.experimental import pallas as pl
from jax.experimental.pallas import tpu as pltpu
from jax.sharding import PartitionSpec as P

MESH = pl.DeviceIdType.MESH
SOIL_STEPS = 4
LB_DEV = 16
CAP_P = 4
LANES = 128
SUBL = 8
CHUNKS = 2
WPARTS = 4
f32 = jnp.float32
bf16 = jnp.bfloat16
i32 = jnp.int32


def iota(shape, dim):
    return lax.broadcasted_iota(i32, shape, dim)


def split_dot(onehot, values):
    high = values.astype(bf16)
    low = (values - high.astype(f32)).astype(bf16)
    return jnp.dot(onehot, high, preferred_element_type=f32) + jnp.dot(
        onehot, low, preferred_element_type=f32
    )


def swap8(regs):
    row = iota((SUBL, LANES), 0)
    regs = list(regs)
    for step in (1, 2, 4):
        keep = (row & step) == 0
        out = list(regs)
        for i in range(8):
            if i & step == 0:
                a, b = regs[i], regs[i + step]
                out[i] = jnp.where(keep, a, pltpu.roll(b, step, 0))
                out[i + step] = jnp.where(keep, pltpu.roll(a, SUBL - step, 0), b)
        regs = out
    return regs


def softplus(x):
    return jnp.maximum(x, 0.0) + jnp.log1p(jnp.exp(-jnp.abs(x)))


def sigmoid(x):
    return 1.0 / (1.0 + jnp.exp(-x))


def kernel(
    tiles, subs, capacity,
    atm_h, pair_atm_h, pair_land_h, owner_h, mask_h, w_hbm, c_hbm, m_hbm,
    forcing_v, soil_v, river_v, number_v,
    atm, pair_atm, pair_land, owner, mask,
    w_v, c_raw, m_raw, ct, mt, gt, rt, it, ut, fwd, unit_v, edge_s, edge_r, meta_s, meta_r,
    slot_s, slot_r, num_s, num_r, val_s, val_r, pick_v, pbuf, amat, bmat, rmat, runoff, drain, drain_u,
    in_sem, w_sem, cm_sem, edge_ss, edge_rs, meta_ss, meta_rs, slot_ss, slot_rs,
    num_ss, num_rs, val_ss, val_rs,
):
    t = lax.axis_index("tile")
    s = lax.axis_index("sub")
    fields = atm.shape[0]
    pairs = w_hbm.shape[0]
    width = w_hbm.shape[3]
    cols = width // CHUNKS
    layers = c_hbm.shape[0]
    blocks = owner.shape[1]
    slab = CAP_P * fields
    prows = pairs * SUBL
    nslot = 3 * subs * slab
    per_part = pairs // WPARTS
    padcap = val_s.shape[1]

    near = []
    for i in range(subs):
        for o in (0, 2):
            near.append((o, lax.rem(s + i, subs)))
    for i in range(1, subs):
        near.append((1, lax.rem(s + i, subs)))
    partners = [(lax.rem(t + o - 1 + tiles, tiles), ds) for o, ds in near]
    far = [lax.rem(t + i, tiles) for i in range(1, tiles)]
    everyone = partners + [(far[i - 1], s) for i in range(2, tiles - 1)]
    barrier = pltpu.get_barrier_semaphore()
    for who in everyone:
        pl.semaphore_signal(barrier, inc=1, device_id=who, device_id_type=MESH)
    in_copies = []
    for k, (src, dst) in enumerate(
        ((atm_h, atm), (pair_atm_h, pair_atm), (pair_land_h, pair_land), (owner_h, owner), (mask_h, mask))
    ):
        copy = pltpu.make_async_copy(src, dst, in_sem.at[k])
        copy.start()
        in_copies.append(copy)
    w_copies = []
    for c in range(CHUNKS):
        for g in range(WPARTS):
            part = pl.ds(g * per_part, per_part)
            copy = pltpu.make_async_copy(
                w_hbm.at[part, :, :, pl.ds(c * cols, cols)], w_v.at[c, part], w_sem.at[c, g]
            )
            copy.start()
            w_copies.append(copy)
    c_copy = pltpu.make_async_copy(c_hbm, c_raw, cm_sem.at[0])
    m_copy = pltpu.make_async_copy(m_hbm, m_raw, cm_sem.at[1])
    c_copy.start()
    m_copy.start()

    for copy in in_copies:
        copy.wait()
    edge_s[0, 0:fields, :] = atm[:, SUBL - 1, :]
    edge_s[1, 0:fields, :] = atm[:, 0, :]
    pl.semaphore_wait(barrier, len(everyone))

    me = t * subs + s
    total = tiles * subs
    edge_copies = []
    for k, to in enumerate((lax.rem(me + 1, total), lax.rem(me + total - 1, total))):
        copy = pltpu.make_async_remote_copy(
            src_ref=edge_s.at[k], dst_ref=edge_r.at[k], send_sem=edge_ss.at[k], recv_sem=edge_rs.at[k],
            device_id=(to // subs, lax.rem(to, subs)), device_id_type=MESH,
        )
        copy.start()
        edge_copies.append(copy)

    prow = iota((prows, pairs), 0) >> 3
    plane = iota((prows, pairs), 1)
    mine = prow == plane
    land = pair_land[...]
    device = land // LB_DEV
    offset = (device // subs - t + 1 + tiles) % tiles
    group = (offset * subs + device % subs).astype(f32)
    atm_row = pair_atm[...].astype(f32)
    local = (land % LB_DEV).astype(f32)

    def column(row):
        return jnp.sum(jnp.where(mine, row, 0.0), axis=1, keepdims=True)

    group_col = column(group)
    rank_col = jnp.sum(
        jnp.where((group == group_col) & (plane < prow), 1.0, 0.0), axis=1, keepdims=True
    )
    atm_col = column(atm_row).astype(i32)
    local_col = column(local)
    f_col = iota((prows, 1), 0) & 7
    real = f_col < fields
    group_i = group_col.astype(i32)
    rank_i = rank_col.astype(i32)
    slot_col = jnp.where(real, (group_i * CAP_P + rank_i) * fields + f_col, -1)
    a_t = jnp.where(iota((prows, nslot), 1) == slot_col, 1.0, 0.0)
    amat[...] = jnp.transpose(a_t).astype(bf16)
    ngroup = meta_s.shape[0]
    g_t = jnp.where(iota((prows, LANES), 1) == group_i, 1.0, 0.0)
    code = (f_col * LB_DEV).astype(f32) + local_col + 1.0
    q_t = jnp.where((iota((prows, LANES), 1) == rank_i * fields + f_col) & real, code, 0.0)
    metas = jnp.dot(
        jnp.transpose(g_t).astype(bf16), q_t.astype(bf16), preferred_element_type=f32
    )
    for g in range(ngroup):
        meta_s[g] = jnp.broadcast_to(metas[g : g + 1, :], (SUBL, LANES))
    own = subs + s

    def sends(src, dst, ssem, rsem):
        for (o, ds), who in zip(near, partners):
            pltpu.make_async_remote_copy(
                src_ref=src.at[o * subs + ds], dst_ref=dst.at[o * subs + s],
                send_sem=ssem, recv_sem=rsem, device_id=who, device_id_type=MESH,
            ).start()

    def all_bytes(ref, count, sem):
        part = ref.at[pl.ds(0, count)]
        pltpu.make_async_copy(part, part, sem).wait()

    sends(meta_s, meta_r, meta_ss, meta_rs)
    meta_r[pl.ds(own, 1)] = meta_s[pl.ds(own, 1)]

    cell = atm[...].reshape(fields * SUBL, LANES)
    lane = iota(cell.shape, 1)
    arow = iota(cell.shape, 0) & 7
    right = pltpu.roll(cell, LANES - 1, 1)
    left = pltpu.roll(cell, 1, 1)
    grad_x = jnp.where(
        lane == 0, right - cell, jnp.where(lane == LANES - 1, cell - left, (right - left) * 0.5)
    )
    pick = jnp.where(
        iota((prows, fields * SUBL), 1) == f_col * SUBL + atm_col, 1.0, 0.0
    ).astype(bf16)
    pick_v[:, 0 : 2 * LANES] = jnp.dot(
        pick, jnp.concatenate([cell, grad_x], axis=1).astype(bf16), preferred_element_type=f32
    )
    def first_products(c):
        for g in range(WPARTS):
            w_copies[c * WPARTS + g].wait()
            parts = []
            for p in range(g * per_part, (g + 1) * per_part):
                rows = pick_v[p * SUBL : (p + 1) * SUBL, 0 : 2 * LANES].astype(bf16)
                parts.append(jnp.dot(
                    rows, w_v[c, p, 0:2].reshape(2 * LANES, cols), preferred_element_type=f32
                ))
            pbuf[c, g * per_part * SUBL : (g + 1) * per_part * SUBL, :] = jnp.concatenate(
                parts, axis=0
            )

    first_products(0)
    for copy in edge_copies:
        copy.wait()
    before = jnp.concatenate(
        [jnp.broadcast_to(edge_r[0, f : f + 1, :], (SUBL, LANES)) for f in range(fields)], axis=0
    )
    after = jnp.concatenate(
        [jnp.broadcast_to(edge_r[1, f : f + 1, :], (SUBL, LANES)) for f in range(fields)], axis=0
    )
    down = jnp.where(arow == SUBL - 1, after, pltpu.roll(cell, fields * SUBL - 1, 0))
    up = jnp.where(arow == 0, before, pltpu.roll(cell, 1, 0))
    grad_y = (down - up) * 0.5
    pick_v[:, 2 * LANES :] = jnp.dot(pick, grad_y.astype(bf16), preferred_element_type=f32)

    for c in range(CHUNKS):
        if c > 0:
            first_products(c)
        parts = []
        for p in range(pairs):
            rows = pick_v[p * SUBL : (p + 1) * SUBL, 2 * LANES :].astype(bf16)
            parts.append(jnp.dot(rows, w_v[c, p, 2], preferred_element_type=f32))
        slots = split_dot(amat[...], pbuf[c] + jnp.concatenate(parts, axis=0))
        slot_s[c] = slots.reshape(3 * subs, slab, cols)
        sends(slot_s.at[c], slot_r.at[c], slot_ss.at[c], slot_rs.at[c])
        slot_r[c, pl.ds(own, 1)] = slot_s[c, pl.ds(own, 1)]

    k_row = iota((blocks, blocks), 0)
    natural = (k_row & (LB_DEV - 1)) * (blocks // LB_DEV) + k_row // LB_DEV
    j_lane = iota((blocks, blocks), 1)
    own_row = owner[...].astype(f32)
    own_col = jnp.sum(jnp.where(j_lane == natural, own_row, 0.0), axis=1, keepdims=True)
    river_rank = jnp.sum(
        jnp.where((own_row == own_col) & (j_lane < natural), 1.0, 0.0), axis=1, keepdims=True
    ).astype(i32)
    own_i = own_col.astype(i32)
    r_t = jnp.where(iota((blocks, tiles * padcap), 1) == own_i * padcap + river_rank, 1.0, 0.0)
    rmat[...] = jnp.transpose(r_t).astype(bf16)
    o_t = jnp.where(iota((blocks, LANES), 1) == own_i, 1.0, 0.0)
    n_t = jnp.where(
        iota((blocks, LANES), 1) == river_rank, natural[:, 0:1].astype(f32) + 1.0, 0.0
    )
    numbers = jnp.dot(
        jnp.transpose(o_t).astype(bf16), n_t.astype(bf16), preferred_element_type=f32
    )
    for to in range(tiles):
        num_s[to] = jnp.broadcast_to(numbers[to : to + 1, :], (SUBL, LANES))

    def river_sends(src, dst, ssem, rsem):
        for to in far:
            pltpu.make_async_remote_copy(
                src_ref=src.at[to], dst_ref=dst.at[t], send_sem=ssem, recv_sem=rsem,
                device_id=(to, s), device_id_type=MESH,
            ).start()
        dst[pl.ds(t, 1)] = src[pl.ds(t, 1)]

    river_sends(num_s, num_r, num_ss, num_rs)

    groups = width // LANES
    c_copy.wait()
    m_copy.wait()

    def place(q, half, b):
        return pl.ds((half * SUBL + b) * width + q * LANES, LANES)

    for raw, out in ((c_raw, ct), (m_raw, mt)):
        for q in range(groups):
            for half in range(LB_DEV // SUBL):
                for k0 in range(0, layers, SUBL):
                    n = min(SUBL, layers - k0)
                    regs = []
                    for b in range(SUBL):
                        part = raw[k0 : k0 + n, place(q, half, b)]
                        if n < SUBL:
                            part = jnp.concatenate(
                                [part, jnp.zeros((SUBL - n, LANES), f32)], axis=0
                            )
                        regs.append(part)
                    regs = swap8(regs)
                    r0 = q * LB_DEV + half * SUBL
                    for k in range(n):
                        out[k0 + k, r0 : r0 + SUBL, :] = regs[k]
    inverse = None
    for k in range(layers):
        diagonal = 1.0 + ct[k]
        if k > 0:
            before_c = ct[k - 1]
            diagonal = diagonal + before_c - before_c * before_c * inverse
        inverse = 1.0 / diagonal
        it[k] = inverse
        rt[k] = ct[k] * inverse
        if k > 0:
            gt[k] = before_c * inverse

    all_bytes(meta_r, len(near), meta_rs)
    spot = iota((slab, LANES), 0) == iota((slab, LANES), 1)
    for g in range(ngroup):
        row = jnp.broadcast_to(meta_r[g, 0:1, :], (slab, LANES))
        got = jnp.sum(jnp.where(spot, row, 0.0), axis=1, keepdims=True).astype(i32) - 1
        second = jnp.where(got < 0, -1, (got & (LB_DEV - 1)) * SUBL + (got >> 4))
        wide = iota((slab, LANES), 1)
        bmat[g * slab : (g + 1) * slab, 0:LANES] = jnp.where(wide == got, 1.0, 0.0)
        bmat[g * slab : (g + 1) * slab, LANES : 2 * LANES] = jnp.where(wide == second, 1.0, 0.0)
    b_all = jnp.transpose(bmat[...]).astype(bf16)

    half_rows = LB_DEV * cols // LANES
    for c in range(CHUNKS):
        here = slice(c * half_rows, (c + 1) * half_rows)
        for step in range(SOIL_STEPS):
            plain = mt[0, here, :] * it[0, here, :]
            if step == 0:
                unit = it[0, here, :]
            else:
                unit = (ut[0, here, :] + 1.0) * it[0, here, :]
            fwd[0, 0] = plain
            fwd[1, 0] = unit
            for k in range(1, layers):
                g = gt[k, here, :]
                inv = it[k, here, :]
                plain = mt[k, here, :] * inv + g * plain
                unit = g * unit if step == 0 else ut[k, here, :] * inv + g * unit
                fwd[0, k] = plain
                fwd[1, k] = unit
            bottom = ct[layers - 1, here, :]
            if step == 0:
                drain[here, :] = bottom * plain
                drain_u[here, :] = bottom * unit
            else:
                drain[here, :] += bottom * plain
                drain_u[here, :] += bottom * unit
            mt[layers - 1, here, :] = plain
            ut[layers - 1, here, :] = unit
            for k in range(layers - 2, -1, -1):
                r = rt[k, here, :]
                plain = fwd[0, k] + r * plain
                unit = fwd[1, k] + r * unit
                mt[k, here, :] = plain
                ut[k, here, :] = unit
    for src, dst in ((mt, soil_v), (ut, unit_v)):
        for q in range(groups):
            for half in range(LB_DEV // SUBL):
                r0 = q * LB_DEV + half * SUBL
                for k0 in range(0, layers, SUBL):
                    n = min(SUBL, layers - k0)
                    regs = [src[k0 + min(k, n - 1), r0 : r0 + SUBL, :] for k in range(SUBL)]
                    regs = swap8(regs)
                    for b in range(SUBL):
                        dst[k0 : k0 + n, place(q, half, b)] = regs[b][:n, :]

    for c in range(CHUNKS):
        all_bytes(slot_r.at[c], len(near), slot_rs.at[c])
        sums = split_dot(b_all, slot_r[c].reshape(nslot, cols))

        def field(f):
            part = sums[f * LB_DEV : (f + 1) * LB_DEV, :]
            return jnp.concatenate(
                [part[:, q * LANES : (q + 1) * LANES] for q in range(cols // LANES)], axis=0
            )

        wet = jnp.concatenate(
            [
                mask[pl.ds(c * (cols // LANES) + q, LB_DEV, stride=groups), :]
                for q in range(cols // LANES)
            ],
            axis=0,
        ).astype(f32)
        soft = softplus(field(0))
        share = sigmoid(field(1))
        source = wet * (soft * share - 0.5 * sigmoid(field(2)) * softplus(field(3)))
        surface = wet * soft * (1.0 - share)
        here = slice(c * half_rows, (c + 1) * half_rows)
        drainage = drain[here, :] + source * drain_u[here, :]
        runoff[here, :] = wet * (SOIL_STEPS * surface + drainage)
        if c == CHUNKS - 1:
            values = split_dot(rmat[...], runoff[...])
            val_s[...] = values.reshape(tiles, padcap, LANES)
            river_sends(val_s, val_r, val_ss, val_rs)
        for b in range(LB_DEV):
            forcing_v[:, b * width + c * cols : b * width + (c + 1) * cols] = sums[
                LANES + b * SUBL : LANES + b * SUBL + fields, :
            ].astype(bf16)
        for q in range(cols // LANES):
            for b in range(LB_DEV):
                at = place(c * (cols // LANES) + q, 0, b)
                row = source[q * LB_DEV + b : q * LB_DEV + b + 1, :]
                soil_v[:, at] += jnp.broadcast_to(row, (layers, LANES)) * unit_v[:, at]
    all_bytes(num_r, len(far), num_rs)
    got = num_r[:, 0, :].astype(i32)[:, :capacity]
    base = (iota(got.shape, 0) * subs + s) * blocks
    number_v[...] = jnp.where(got > 0, got - 1 + base, -1)
    all_bytes(meta_s, len(near), meta_ss)
    for c in range(CHUNKS):
        all_bytes(slot_s.at[c], len(near), slot_ss.at[c])
    all_bytes(num_s, len(far), num_ss)
    all_bytes(val_r, len(far), val_rs)
    river_v[...] = val_r[...]
    all_bytes(val_s, len(far), val_ss)


def hand_on(*refs):
    count = (len(refs) - 1) // 2
    sem = refs[-1]
    copies = []
    for k in range(count):
        copies.append(pltpu.make_async_copy(refs[k], refs[count + k], sem.at[k]))
        copies[-1].start()
    for copy in copies:
        copy.wait()


def on_device(
    tiles, subs, atm_fields, pair_atm, pair_land, pair_weight, land_mask, conductance, soil_moisture,
    river_owner,
):
    fields = atm_fields.shape[0]
    pairs = pair_atm.shape[0]
    layers, cells = conductance.shape
    blocks = river_owner.shape[0]
    width = pair_weight.shape[3]
    cols = width // CHUNKS
    capacity = max(2, 2 * blocks // tiles)
    padcap = -(-capacity // SUBL) * SUBL
    groups = 3 * subs
    slab = CAP_P * fields
    rows = cells // LANES
    dma = pltpu.SemaphoreType.DMA
    hbm = pl.BlockSpec(memory_space=pltpu.HBM)
    inside = pl.BlockSpec(memory_space=pltpu.VMEM)
    half_rows = rows // CHUNKS
    shapes = (
        ((fields, cells), bf16),
        ((layers, cells), f32),
        ((tiles, padcap, LANES), f32),
        ((tiles, capacity), i32),
    )
    column = pltpu.VMEM((layers, rows, LANES), f32)
    results = pl.pallas_call(
        functools.partial(kernel, tiles, subs, capacity),
        out_shape=[pltpu.VMEM(*shape) for shape in shapes],
        in_specs=[hbm] * 8,
        out_specs=[inside] * 4,
        scratch_shapes=[
            pltpu.VMEM(atm_fields.shape, f32),
            pltpu.VMEM((1, pairs), i32),
            pltpu.VMEM((1, pairs), i32),
            pltpu.VMEM((1, blocks), i32),
            pltpu.VMEM((rows, LANES), i32),
            pltpu.VMEM((CHUNKS, pairs, 3, LANES, cols), bf16),
            pltpu.VMEM((layers, cells), f32),
            pltpu.VMEM((layers, cells), f32),
            column,
            column,
            column,
            column,
            column,
            column,
            pltpu.VMEM((2, layers, half_rows, LANES), f32),
            pltpu.VMEM((layers, cells), f32),
            pltpu.VMEM((2, SUBL, LANES), f32),
            pltpu.VMEM((2, SUBL, LANES), f32),
            pltpu.VMEM((groups, SUBL, LANES), f32),
            pltpu.VMEM((groups, SUBL, LANES), f32),
            pltpu.VMEM((CHUNKS, groups, slab, cols), f32),
            pltpu.VMEM((CHUNKS, groups, slab, cols), f32),
            pltpu.VMEM((tiles, SUBL, LANES), f32),
            pltpu.VMEM((tiles, SUBL, LANES), f32),
            pltpu.VMEM((tiles, padcap, LANES), f32),
            pltpu.VMEM((tiles, padcap, LANES), f32),
            pltpu.VMEM((pairs * SUBL, 3 * LANES), f32),
            pltpu.VMEM((CHUNKS, pairs * SUBL, cols), f32),
            pltpu.VMEM((groups * slab, pairs * SUBL), bf16),
            pltpu.VMEM((groups * slab, 2 * LANES), f32),
            pltpu.VMEM((tiles * padcap, blocks), bf16),
            pltpu.VMEM((rows, LANES), f32),
            pltpu.VMEM((rows, LANES), f32),
            pltpu.VMEM((rows, LANES), f32),
            dma((5,)),
            dma((CHUNKS, WPARTS)),
            dma((2,)),
            dma((2,)),
            dma((2,)),
            dma(()),
            dma(()),
            dma((CHUNKS,)),
            dma((CHUNKS,)),
            dma(()),
            dma(()),
            dma(()),
            dma(()),
        ],
        compiler_params=pltpu.CompilerParams(
            collective_id=0, has_side_effects=True, vmem_limit_bytes=48 * 2**20
        ),
    )(
        *(
            pltpu.with_memory_space_constraint(array, pltpu.HBM)
            for array in (
                atm_fields, pair_atm.reshape(1, pairs), pair_land.reshape(1, pairs),
                river_owner.reshape(1, blocks), land_mask.reshape(rows, LANES),
                pair_weight, conductance, soil_moisture,
            )
        )
    )
    forcing, soil, values, numbers = pl.pallas_call(
        hand_on,
        out_shape=[jax.ShapeDtypeStruct(*shape) for shape in shapes],
        in_specs=[pl.BlockSpec(memory_space=pl.ANY)] * 4,
        out_specs=[hbm] * 4,
        scratch_shapes=[dma((4,))],
        compiler_params=pltpu.CompilerParams(vmem_limit_bytes=16 * 2**20),
    )(*(pltpu.with_memory_space_constraint(array, pltpu.VMEM) for array in results))
    return (forcing, soil, values[None, None, :, :capacity, :], numbers[None, None])


def solution(mesh):
    both = ("tile", "sub")
    return jax.shard_map(
        functools.partial(on_device, mesh.shape["tile"], mesh.shape["sub"]),
        mesh=mesh,
        in_specs=(
            P(None, both, None),
            P(both),
            P(both),
            P(both, None, None, None),
            P(both),
            P(None, both),
            P(None, both),
            P(both),
        ),
        out_specs=(
            P(None, both),
            P(None, both),
            P("tile", "sub", None, None, None),
            P("tile", "sub", None, None),
        ),
        check_vma=False,
    )
```

```python
import functools

import jax
import jax.numpy as jnp
from jax import lax
from jax.experimental import pallas as pl
from jax.experimental.pallas import tpu as pltpu
from jax.sharding import PartitionSpec as P

MESH = pl.DeviceIdType.MESH
SOIL_STEPS = 4
LB_DEV = 16
CAP_P = 4
LANES = 128
SUBL = 8
CHUNKS = 2
WPARTS = 4
f32 = jnp.float32
bf16 = jnp.bfloat16
i32 = jnp.int32


def iota(shape, dim):
    return lax.broadcasted_iota(i32, shape, dim)


def split_dot(onehot, values):
    high = values.astype(bf16)
    low = (values - high.astype(f32)).astype(bf16)
    return jnp.dot(onehot, high, preferred_element_type=f32) + jnp.dot(
        onehot, low, preferred_element_type=f32
    )


def swap8(regs):
    row = iota((SUBL, LANES), 0)
    regs = list(regs)
    for step in (1, 2, 4):
        keep = (row & step) == 0
        out = list(regs)
        for i in range(8):
            if i & step == 0:
                a, b = regs[i], regs[i + step]
                out[i] = jnp.where(keep, a, pltpu.roll(b, step, 0))
                out[i + step] = jnp.where(keep, pltpu.roll(a, SUBL - step, 0), b)
        regs = out
    return regs


def softplus(x):
    return jnp.maximum(x, 0.0) + jnp.log1p(jnp.exp(-jnp.abs(x)))


def sigmoid(x):
    return 1.0 / (1.0 + jnp.exp(-x))


def kernel(
    tiles, subs, capacity,
    atm_h, pair_atm_h, pair_land_h, owner_h, mask_h, w_hbm, c_hbm, m_hbm,
    forcing_v, soil_v, river_v, number_v,
    atm, pair_atm, pair_land, owner, mask,
    w_v, c_raw, m_raw, ct, mt, gt, rt, it, ut, fwd, unit_v, edge_s, edge_r, meta_s, meta_r,
    slot_s, slot_r, num_s, num_r, val_s, val_r, pick_v, pbuf, amat, bmat, rmat, runoff, drain, drain_u,
    in_sem, w_sem, cm_sem, edge_ss, edge_rs, meta_ss, meta_rs, slot_ss, slot_rs,
    num_ss, num_rs, val_ss, val_rs,
):
    t = lax.axis_index("tile")
    s = lax.axis_index("sub")
    fields = atm.shape[0]
    pairs = w_hbm.shape[0]
    width = w_hbm.shape[3]
    cols = width // CHUNKS
    layers = c_hbm.shape[0]
    blocks = owner.shape[1]
    slab = CAP_P * fields
    prows = pairs * SUBL
    nslot = 3 * subs * slab
    per_part = pairs // WPARTS
    padcap = val_s.shape[1]

    near = []
    for i in range(subs):
        for o in (0, 2):
            near.append((o, lax.rem(s + i, subs)))
    for i in range(1, subs):
        near.append((1, lax.rem(s + i, subs)))
    partners = [(lax.rem(t + o - 1 + tiles, tiles), ds) for o, ds in near]
    far = [lax.rem(t + i, tiles) for i in range(1, tiles)]
    everyone = partners + [(far[i - 1], s) for i in range(2, tiles - 1)]
    barrier = pltpu.get_barrier_semaphore()
    for who in everyone:
        pl.semaphore_signal(barrier, inc=1, device_id=who, device_id_type=MESH)
    in_copies = []
    for k, (src, dst) in enumerate(
        ((atm_h, atm), (pair_atm_h, pair_atm), (pair_land_h, pair_land), (owner_h, owner), (mask_h, mask))
    ):
        copy = pltpu.make_async_copy(src, dst, in_sem.at[k])
        copy.start()
        in_copies.append(copy)
    w_copies = []
    for c in range(CHUNKS):
        for g in range(WPARTS):
            part = pl.ds(g * per_part, per_part)
            copy = pltpu.make_async_copy(
                w_hbm.at[part, :, :, pl.ds(c * cols, cols)], w_v.at[c, part], w_sem.at[c, g]
            )
            if c == 0:
                copy.start()
            w_copies.append(copy)
    c_copy = pltpu.make_async_copy(c_hbm, c_raw, cm_sem.at[0])
    m_copy = pltpu.make_async_copy(m_hbm, m_raw, cm_sem.at[1])
    for copy in in_copies:
        copy.wait()
    edge_s[0, 0:fields, :] = atm[:, SUBL - 1, :]
    edge_s[1, 0:fields, :] = atm[:, 0, :]
    pl.semaphore_wait(barrier, len(everyone))

    me = t * subs + s
    total = tiles * subs
    edge_copies = []
    for k, to in enumerate((lax.rem(me + 1, total), lax.rem(me + total - 1, total))):
        copy = pltpu.make_async_remote_copy(
            src_ref=edge_s.at[k], dst_ref=edge_r.at[k], send_sem=edge_ss.at[k], recv_sem=edge_rs.at[k],
            device_id=(to // subs, lax.rem(to, subs)), device_id_type=MESH,
        )
        copy.start()
        edge_copies.append(copy)

    prow = iota((prows, pairs), 0) >> 3
    plane = iota((prows, pairs), 1)
    mine = prow == plane
    land = pair_land[...]
    device = land // LB_DEV
    offset = (device // subs - t + 1 + tiles) % tiles
    group = (offset * subs + device % subs).astype(f32)
    atm_row = pair_atm[...].astype(f32)
    local = (land % LB_DEV).astype(f32)

    def column(row):
        return jnp.sum(jnp.where(mine, row, 0.0), axis=1, keepdims=True)

    group_col = column(group)
    rank_col = jnp.sum(
        jnp.where((group == group_col) & (plane < prow), 1.0, 0.0), axis=1, keepdims=True
    )
    atm_col = column(atm_row).astype(i32)
    local_col = column(local)
    f_col = iota((prows, 1), 0) & 7
    real = f_col < fields
    group_i = group_col.astype(i32)
    rank_i = rank_col.astype(i32)
    slot_col = jnp.where(real, (group_i * CAP_P + rank_i) * fields + f_col, -1)
    a_t = jnp.where(iota((prows, nslot), 1) == slot_col, 1.0, 0.0)
    amat[...] = jnp.transpose(a_t).astype(bf16)
    own = subs + s

    def sends(src, dst, ssem, rsem):
        for (o, ds), who in zip(near, partners):
            pltpu.make_async_remote_copy(
                src_ref=src.at[o * subs + ds], dst_ref=dst.at[o * subs + s],
                send_sem=ssem, recv_sem=rsem, device_id=who, device_id_type=MESH,
            ).start()

    def all_bytes(ref, count, sem):
        part = ref.at[pl.ds(0, count)]
        pltpu.make_async_copy(part, part, sem).wait()

    cell = atm[...].reshape(fields * SUBL, LANES)
    lane = iota(cell.shape, 1)
    arow = iota(cell.shape, 0) & 7
    right = pltpu.roll(cell, LANES - 1, 1)
    left = pltpu.roll(cell, 1, 1)
    grad_x = jnp.where(
        lane == 0, right - cell, jnp.where(lane == LANES - 1, cell - left, (right - left) * 0.5)
    )
    pick = jnp.where(
        iota((prows, fields * SUBL), 1) == f_col * SUBL + atm_col, 1.0, 0.0
    ).astype(bf16)
    pick_v[:, 0 : 2 * LANES] = jnp.dot(
        pick, jnp.concatenate([cell, grad_x], axis=1).astype(bf16), preferred_element_type=f32
    )
    def first_products(c):
        for g in range(WPARTS):
            w_copies[c * WPARTS + g].wait()
            if c + 1 < CHUNKS:
                w_copies[(c + 1) * WPARTS + g].start()
            parts = []
            for p in range(g * per_part, (g + 1) * per_part):
                rows = pick_v[p * SUBL : (p + 1) * SUBL, 0 : 2 * LANES].astype(bf16)
                parts.append(jnp.dot(
                    rows, w_v[c, p, 0:2].reshape(2 * LANES, cols), preferred_element_type=f32
                ))
            pbuf[c, g * per_part * SUBL : (g + 1) * per_part * SUBL, :] = jnp.concatenate(
                parts, axis=0
            )

    first_products(0)
    c_copy.start()
    m_copy.start()
    for copy in edge_copies:
        copy.wait()
    before = jnp.concatenate(
        [jnp.broadcast_to(edge_r[0, f : f + 1, :], (SUBL, LANES)) for f in range(fields)], axis=0
    )
    after = jnp.concatenate(
        [jnp.broadcast_to(edge_r[1, f : f + 1, :], (SUBL, LANES)) for f in range(fields)], axis=0
    )
    down = jnp.where(arow == SUBL - 1, after, pltpu.roll(cell, fields * SUBL - 1, 0))
    up = jnp.where(arow == 0, before, pltpu.roll(cell, 1, 0))
    grad_y = (down - up) * 0.5
    pick_v[:, 2 * LANES :] = jnp.dot(pick, grad_y.astype(bf16), preferred_element_type=f32)

    for c in range(CHUNKS):
        if c > 0:
            first_products(c)
        parts = []
        for p in range(pairs):
            rows = pick_v[p * SUBL : (p + 1) * SUBL, 2 * LANES :].astype(bf16)
            parts.append(jnp.dot(rows, w_v[c, p, 2], preferred_element_type=f32))
        slots = split_dot(amat[...], pbuf[c] + jnp.concatenate(parts, axis=0))
        slot_s[c] = slots.reshape(3 * subs, slab, cols)
        sends(slot_s.at[c], slot_r.at[c], slot_ss.at[c], slot_rs.at[c])
        slot_r[c, pl.ds(own, 1)] = slot_s[c, pl.ds(own, 1)]

    ngroup = meta_s.shape[0]
    g_t = jnp.where(iota((prows, LANES), 1) == group_i, 1.0, 0.0)
    code = (f_col * LB_DEV).astype(f32) + local_col + 1.0
    q_t = jnp.where((iota((prows, LANES), 1) == rank_i * fields + f_col) & real, code, 0.0)
    metas = jnp.dot(
        jnp.transpose(g_t).astype(bf16), q_t.astype(bf16), preferred_element_type=f32
    )
    for g in range(ngroup):
        meta_s[g] = jnp.broadcast_to(metas[g : g + 1, :], (SUBL, LANES))
    sends(meta_s, meta_r, meta_ss, meta_rs)
    meta_r[pl.ds(own, 1)] = meta_s[pl.ds(own, 1)]

    k_row = iota((blocks, blocks), 0)
    natural = (k_row & (LB_DEV - 1)) * (blocks // LB_DEV) + k_row // LB_DEV
    j_lane = iota((blocks, blocks), 1)
    own_row = owner[...].astype(f32)
    own_col = jnp.sum(jnp.where(j_lane == natural, own_row, 0.0), axis=1, keepdims=True)
    river_rank = jnp.sum(
        jnp.where((own_row == own_col) & (j_lane < natural), 1.0, 0.0), axis=1, keepdims=True
    ).astype(i32)
    own_i = own_col.astype(i32)
    r_t = jnp.where(iota((blocks, tiles * padcap), 1) == own_i * padcap + river_rank, 1.0, 0.0)
    rmat[...] = jnp.transpose(r_t).astype(bf16)
    o_t = jnp.where(iota((blocks, LANES), 1) == own_i, 1.0, 0.0)
    n_t = jnp.where(
        iota((blocks, LANES), 1) == river_rank, natural[:, 0:1].astype(f32) + 1.0, 0.0
    )
    numbers = jnp.dot(
        jnp.transpose(o_t).astype(bf16), n_t.astype(bf16), preferred_element_type=f32
    )
    for to in range(tiles):
        num_s[to] = jnp.broadcast_to(numbers[to : to + 1, :], (SUBL, LANES))

    def river_sends(src, dst, ssem, rsem):
        for to in far:
            pltpu.make_async_remote_copy(
                src_ref=src.at[to], dst_ref=dst.at[t], send_sem=ssem, recv_sem=rsem,
                device_id=(to, s), device_id_type=MESH,
            ).start()
        dst[pl.ds(t, 1)] = src[pl.ds(t, 1)]

    river_sends(num_s, num_r, num_ss, num_rs)

    groups = width // LANES
    c_copy.wait()
    m_copy.wait()

    def place(q, half, b):
        return pl.ds((half * SUBL + b) * width + q * LANES, LANES)

    for raw, out in ((c_raw, ct), (m_raw, mt)):
        for q in range(groups):
            for half in range(LB_DEV // SUBL):
                for k0 in range(0, layers, SUBL):
                    n = min(SUBL, layers - k0)
                    regs = []
                    for b in range(SUBL):
                        part = raw[k0 : k0 + n, place(q, half, b)]
                        if n < SUBL:
                            part = jnp.concatenate(
                                [part, jnp.zeros((SUBL - n, LANES), f32)], axis=0
                            )
                        regs.append(part)
                    regs = swap8(regs)
                    r0 = q * LB_DEV + half * SUBL
                    for k in range(n):
                        out[k0 + k, r0 : r0 + SUBL, :] = regs[k]
    inverse = None
    for k in range(layers):
        diagonal = 1.0 + ct[k]
        if k > 0:
            before_c = ct[k - 1]
            diagonal = diagonal + before_c - before_c * before_c * inverse
        inverse = 1.0 / diagonal
        it[k] = inverse
        rt[k] = ct[k] * inverse
        if k > 0:
            gt[k] = before_c * inverse

    all_bytes(meta_r, len(near), meta_rs)
    spot = iota((slab, LANES), 0) == iota((slab, LANES), 1)
    for g in range(ngroup):
        row = jnp.broadcast_to(meta_r[g, 0:1, :], (slab, LANES))
        got = jnp.sum(jnp.where(spot, row, 0.0), axis=1, keepdims=True).astype(i32) - 1
        second = jnp.where(got < 0, -1, (got & (LB_DEV - 1)) * SUBL + (got >> 4))
        wide = iota((slab, LANES), 1)
        bmat[g * slab : (g + 1) * slab, 0:LANES] = jnp.where(wide == got, 1.0, 0.0)
        bmat[g * slab : (g + 1) * slab, LANES : 2 * LANES] = jnp.where(wide == second, 1.0, 0.0)
    b_all = jnp.transpose(bmat[...]).astype(bf16)

    half_rows = LB_DEV * cols // LANES
    for c in range(CHUNKS):
        here = slice(c * half_rows, (c + 1) * half_rows)
        for step in range(SOIL_STEPS):
            plain = mt[0, here, :] * it[0, here, :]
            if step == 0:
                unit = it[0, here, :]
            else:
                unit = (ut[0, here, :] + 1.0) * it[0, here, :]
            fwd[0, 0] = plain
            fwd[1, 0] = unit
            for k in range(1, layers):
                g = gt[k, here, :]
                inv = it[k, here, :]
                plain = mt[k, here, :] * inv + g * plain
                unit = g * unit if step == 0 else ut[k, here, :] * inv + g * unit
                fwd[0, k] = plain
                fwd[1, k] = unit
            bottom = ct[layers - 1, here, :]
            if step == 0:
                drain[here, :] = bottom * plain
                drain_u[here, :] = bottom * unit
            else:
                drain[here, :] += bottom * plain
                drain_u[here, :] += bottom * unit
            mt[layers - 1, here, :] = plain
            ut[layers - 1, here, :] = unit
            for k in range(layers - 2, -1, -1):
                r = rt[k, here, :]
                plain = fwd[0, k] + r * plain
                unit = fwd[1, k] + r * unit
                mt[k, here, :] = plain
                ut[k, here, :] = unit
    for src, dst in ((mt, soil_v), (ut, unit_v)):
        for q in range(groups):
            for half in range(LB_DEV // SUBL):
                r0 = q * LB_DEV + half * SUBL
                for k0 in range(0, layers, SUBL):
                    n = min(SUBL, layers - k0)
                    regs = [src[k0 + min(k, n - 1), r0 : r0 + SUBL, :] for k in range(SUBL)]
                    regs = swap8(regs)
                    for b in range(SUBL):
                        dst[k0 : k0 + n, place(q, half, b)] = regs[b][:n, :]

    for c in range(CHUNKS):
        all_bytes(slot_r.at[c], len(near), slot_rs.at[c])
        sums = split_dot(b_all, slot_r[c].reshape(nslot, cols))

        def field(f):
            part = sums[f * LB_DEV : (f + 1) * LB_DEV, :]
            return jnp.concatenate(
                [part[:, q * LANES : (q + 1) * LANES] for q in range(cols // LANES)], axis=0
            )

        wet = jnp.concatenate(
            [
                mask[pl.ds(c * (cols // LANES) + q, LB_DEV, stride=groups), :]
                for q in range(cols // LANES)
            ],
            axis=0,
        ).astype(f32)
        soft = softplus(field(0))
        share = sigmoid(field(1))
        source = wet * (soft * share - 0.5 * sigmoid(field(2)) * softplus(field(3)))
        surface = wet * soft * (1.0 - share)
        here = slice(c * half_rows, (c + 1) * half_rows)
        drainage = drain[here, :] + source * drain_u[here, :]
        runoff[here, :] = wet * (SOIL_STEPS * surface + drainage)
        if c == CHUNKS - 1:
            values = split_dot(rmat[...], runoff[...])
            val_s[...] = values.reshape(tiles, padcap, LANES)
            river_sends(val_s, val_r, val_ss, val_rs)
        for b in range(LB_DEV):
            forcing_v[:, b * width + c * cols : b * width + (c + 1) * cols] = sums[
                LANES + b * SUBL : LANES + b * SUBL + fields, :
            ].astype(bf16)
        for q in range(cols // LANES):
            for b in range(LB_DEV):
                at = place(c * (cols // LANES) + q, 0, b)
                row = source[q * LB_DEV + b : q * LB_DEV + b + 1, :]
                soil_v[:, at] += jnp.broadcast_to(row, (layers, LANES)) * unit_v[:, at]
    all_bytes(num_r, len(far), num_rs)
    got = num_r[:, 0, :].astype(i32)[:, :capacity]
    base = (iota(got.shape, 0) * subs + s) * blocks
    number_v[...] = jnp.where(got > 0, got - 1 + base, -1)
    all_bytes(meta_s, len(near), meta_ss)
    for c in range(CHUNKS):
        all_bytes(slot_s.at[c], len(near), slot_ss.at[c])
    all_bytes(num_s, len(far), num_ss)
    all_bytes(val_r, len(far), val_rs)
    river_v[...] = val_r[...]
    all_bytes(val_s, len(far), val_ss)


def hand_on(*refs):
    count = (len(refs) - 1) // 2
    sem = refs[-1]
    copies = []
    parts = sem.shape[0] - count + 1
    length = refs[1].shape[1] // parts
    for k in range(parts):
        part = pl.ds(k * length, length)
        copies.append(
            pltpu.make_async_copy(refs[1].at[:, part], refs[count + 1].at[:, part], sem.at[count - 1 + k])
        )
        copies[-1].start()
    for n, k in enumerate((0, 2, 3)):
        copies.append(pltpu.make_async_copy(refs[k], refs[count + k], sem.at[n]))
        copies[-1].start()
    for copy in copies:
        copy.wait()


def on_device(
    tiles, subs, atm_fields, pair_atm, pair_land, pair_weight, land_mask, conductance, soil_moisture,
    river_owner,
):
    fields = atm_fields.shape[0]
    pairs = pair_atm.shape[0]
    layers, cells = conductance.shape
    blocks = river_owner.shape[0]
    width = pair_weight.shape[3]
    cols = width // CHUNKS
    capacity = max(2, 2 * blocks // tiles)
    padcap = -(-capacity // SUBL) * SUBL
    groups = 3 * subs
    slab = CAP_P * fields
    rows = cells // LANES
    dma = pltpu.SemaphoreType.DMA
    hbm = pl.BlockSpec(memory_space=pltpu.HBM)
    inside = pl.BlockSpec(memory_space=pltpu.VMEM)
    half_rows = rows // CHUNKS
    shapes = (
        ((fields, cells), bf16),
        ((layers, cells), f32),
        ((tiles, padcap, LANES), f32),
        ((tiles, capacity), i32),
    )
    column = pltpu.VMEM((layers, rows, LANES), f32)
    results = pl.pallas_call(
        functools.partial(kernel, tiles, subs, capacity),
        out_shape=[pltpu.VMEM(*shape) for shape in shapes],
        in_specs=[hbm] * 8,
        out_specs=[inside] * 4,
        scratch_shapes=[
            pltpu.VMEM(atm_fields.shape, f32),
            pltpu.VMEM((1, pairs), i32),
            pltpu.VMEM((1, pairs), i32),
            pltpu.VMEM((1, blocks), i32),
            pltpu.VMEM((rows, LANES), i32),
            pltpu.VMEM((CHUNKS, pairs, 3, LANES, cols), bf16),
            pltpu.VMEM((layers, cells), f32),
            pltpu.VMEM((layers, cells), f32),
            column,
            column,
            column,
            column,
            column,
            column,
            pltpu.VMEM((2, layers, half_rows, LANES), f32),
            pltpu.VMEM((layers, cells), f32),
            pltpu.VMEM((2, SUBL, LANES), f32),
            pltpu.VMEM((2, SUBL, LANES), f32),
            pltpu.VMEM((groups, SUBL, LANES), f32),
            pltpu.VMEM((groups, SUBL, LANES), f32),
            pltpu.VMEM((CHUNKS, groups, slab, cols), f32),
            pltpu.VMEM((CHUNKS, groups, slab, cols), f32),
            pltpu.VMEM((tiles, SUBL, LANES), f32),
            pltpu.VMEM((tiles, SUBL, LANES), f32),
            pltpu.VMEM((tiles, padcap, LANES), f32),
            pltpu.VMEM((tiles, padcap, LANES), f32),
            pltpu.VMEM((pairs * SUBL, 3 * LANES), f32),
            pltpu.VMEM((CHUNKS, pairs * SUBL, cols), f32),
            pltpu.VMEM((groups * slab, pairs * SUBL), bf16),
            pltpu.VMEM((groups * slab, 2 * LANES), f32),
            pltpu.VMEM((tiles * padcap, blocks), bf16),
            pltpu.VMEM((rows, LANES), f32),
            pltpu.VMEM((rows, LANES), f32),
            pltpu.VMEM((rows, LANES), f32),
            dma((5,)),
            dma((CHUNKS, WPARTS)),
            dma((2,)),
            dma((2,)),
            dma((2,)),
            dma(()),
            dma(()),
            dma((CHUNKS,)),
            dma((CHUNKS,)),
            dma(()),
            dma(()),
            dma(()),
            dma(()),
        ],
        compiler_params=pltpu.CompilerParams(
            collective_id=0, has_side_effects=True, vmem_limit_bytes=48 * 2**20
        ),
    )(
        *(
            pltpu.with_memory_space_constraint(array, pltpu.HBM)
            for array in (
                atm_fields, pair_atm.reshape(1, pairs), pair_land.reshape(1, pairs),
                river_owner.reshape(1, blocks), land_mask.reshape(rows, LANES),
                pair_weight, conductance, soil_moisture,
            )
        )
    )
    forcing, soil, values, numbers = pl.pallas_call(
        hand_on,
        out_shape=[jax.ShapeDtypeStruct(*shape) for shape in shapes],
        in_specs=[pl.BlockSpec(memory_space=pl.ANY)] * 4,
        out_specs=[hbm] * 4,
        scratch_shapes=[dma((7,))],
        compiler_params=pltpu.CompilerParams(vmem_limit_bytes=16 * 2**20),
    )(*(pltpu.with_memory_space_constraint(array, pltpu.VMEM) for array in results))
    return (forcing, soil, values[None, None, :, :capacity, :], numbers[None, None])


def solution(mesh):
    both = ("tile", "sub")
    return jax.shard_map(
        functools.partial(on_device, mesh.shape["tile"], mesh.shape["sub"]),
        mesh=mesh,
        in_specs=(
            P(None, both, None),
            P(both),
            P(both),
            P(both, None, None, None),
            P(both),
            P(None, both),
            P(None, both),
            P(both),
        ),
        out_specs=(
            P(None, both),
            P(None, both),
            P("tile", "sub", None, None, None),
            P("tile", "sub", None, None),
        ),
        check_vma=False,
    )
```
